256 devices in a mesh: rep: 4 (over x), fsdp: 16 (over z, core), tp: 4 (over y).
Axes of the slice: x: 4, y: 4, z: 8, core: 2. Of those that a mesh axis runs over, the one named last changes fastest.
Arguments:
- weights: float32 [1024, 53248], P('tp', 'fsdp'), may hold values from -0.1875 to 0.1875
- momentum: float32 [4096, 53248], P(('rep', 'tp'), 'fsdp'), may hold values from -6 to 6
- gradient: float32 [4096, 53248], P(('rep', 'tp'), 'fsdp'), may hold values from -120 to 120, as said below
- right_factor: float32 [53248, 256], P('fsdp', 'tp'), may hold values from -6 to 6
Outputs:
- new_weights: float32 [1024, 53248], P('tp', 'fsdp')
- new_momentum: float32 [4096, 53248], P(('rep', 'tp'), 'fsdp')
- new_right: float32 [53248, 256], P('fsdp', 'tp')
The draws below stay inside these ranges and needn't reach their ends.
Inputs may be any that keep to these rules, and one draw needn't show every extreme that they name: `gradient`: finite values.
All inputs are finite; a program needn't handle non-finite values.
Results may differ from the reference program's by a relative error of at most 0.0003.
Values sent between devices are 32-bit elements; how exact they have to be, the bound alone decides.
A program may use at most 128 MiB of HBM per device.

```python
import jax
import jax.numpy as jnp
from jax import lax

RANK = 256
ROWS = 1024
COLS = 53248
REPS = 4


def draw_gradient(key, part):
    key = jax.random.fold_in(key, 7)
    key_vals, key_rows, key_cols = jax.random.split(key, 3)
    shape = (REPS * ROWS, COLS)
    rising = jnp.exp(jnp.log(3.0) * jnp.arange(COLS, dtype=jnp.float32) / COLS)
    values = jnp.clip(jax.random.normal(key_vals, shape, jnp.float32), -4.0, 4.0)
    row_scale = jnp.exp(jax.random.uniform(key_rows, (REPS * ROWS, 1), jnp.float32, jnp.log(0.3), jnp.log(3.0)))
    col_scale = jnp.exp(jax.random.uniform(key_cols, (1, COLS), jnp.float32, jnp.log(0.3), jnp.log(3.0)))
    return values * row_scale * col_scale * rising[None, :]


def steps_of(stream_key, dims, cuts, smallest, high):
    def one(axis_at, blocks):
        draws = jax.random.uniform(jax.random.fold_in(jax.random.fold_in(stream_key, 6), axis_at), (blocks,), jnp.float32, smallest / len(cuts), high / len(cuts))
        return jnp.repeat(jnp.exp(draws), dims[axis_at] // blocks).reshape((-1,) + (1,) * (len(dims) - axis_at - 1))

    gain = one(*cuts[0])
    for cut in cuts[1:]:
        gain = gain * one(*cut)
    return gain


def centred(rng, shape, width, reach, cuts=(), held_as=jnp.bfloat16):
    loudness = steps_of(rng, shape, cuts, -0.22, 0.18) if cuts else 1.0
    entries = jax.random.normal(rng, shape, jnp.float32) * width * loudness
    return jnp.minimum(jnp.maximum(entries, -reach), reach).astype(held_as)


def setup_inputs(seed: int = 0) -> dict:
    splits = jax.random.split(jax.random.key(seed), 5)
    weights = centred(splits[0], (ROWS, COLS), ROWS ** -0.5, 0.1875, ((0, 4), (1, 16)), jnp.float32)
    momentum = centred(splits[1], (REPS * ROWS, COLS), 1.0, 6.0, ((0, 16), (1, 16)), jnp.float32)
    gradient = draw_gradient(jax.random.fold_in(splits[4], 71), 0)
    right_factor = centred(splits[3], (COLS, RANK), 1.0, 6.0, ((0, 16), (1, 4)), jnp.float32)
    return dict(weights=weights, momentum=momentum, gradient=gradient, right_factor=right_factor)


momentum_decay = 0.95
learning_rate = 0.05
norm_eps = 1e-06

def matmul(left_side, right_side):
    return jnp.dot(left_side.astype(jnp.float32), right_side.astype(jnp.float32), preferred_element_type=jnp.float32, precision=lax.Precision.HIGHEST)

def reference(weights, momentum, gradient, right_factor):
    rows = weights.shape[0]
    replicas = momentum.shape[0] // rows
    combined = (momentum + gradient).reshape(replicas, rows, -1)
    left = matmul(combined[0], right_factor)
    for index in range(1, replicas):
        left = left + matmul(combined[index], right_factor)
    left = left / replicas
    gram = matmul(left.T, left)
    lower = jnp.linalg.cholesky(gram)
    ortho = lax.linalg.triangular_solve(lower, left, left_side=False, lower=True, transpose_a=True)
    right_t = matmul(ortho.T, combined[0])
    for index in range(1, replicas):
        right_t = right_t + matmul(ortho.T, combined[index])
    right_t = right_t / replicas
    normal_t = right_t * lax.rsqrt(lax.optimization_barrier(jnp.mean(right_t * right_t, axis=1, keepdims=True)) + norm_eps)
    update = matmul(ortho, right_t)
    new_momentum = (combined - (1.0 - momentum_decay) * update[None]).reshape(replicas * rows, -1)
    new_weights = weights - learning_rate * matmul(ortho, normal_t)
    return (new_weights, new_momentum, normal_t.T)
```

```python
import jax
import jax.numpy as jnp
from jax import lax
from jax.experimental import pallas as pl
from jax.experimental.pallas import tpu as pltpu
from jax.sharding import PartitionSpec as P

MESH = pl.DeviceIdType.MESH
HIGHEST = lax.Precision.HIGHEST
F32 = jnp.float32
BF16 = jnp.bfloat16

momentum_decay = 0.95
learning_rate = 0.05
norm_eps = 1e-06

ROWS = 256
COLS = 3328
CHUNK = 832
EARLY = 512
LATE = CHUNK - EARLY
TOTAL_COLS = 53248
NB = 64
STEP = 8


def dot(a, b, dims=((1,), (0,)), precision=None):
    return lax.dot_general(a, b, (dims, ((), ())), precision=precision, preferred_element_type=F32)


def split(a):
    high = a.astype(BF16)
    return high, (a - high.astype(F32)).astype(BF16)


def dot3(a, b, dims=((1,), (0,))):
    ah, al = split(a)
    bh, bl = split(b)
    return dot(ah, bh, dims) + (dot(ah, bl, dims) + dot(al, bh, dims))


def small_inverse(d):
    rows = lax.broadcasted_iota(jnp.int32, (NB, 128), 0)
    cols = lax.broadcasted_iota(jnp.int32, (NB, 128), 1)
    eye = jnp.where(cols == rows + 64, 1.0, 0.0).astype(F32)
    x = jnp.concatenate([d, jnp.zeros((NB, 128 - NB), F32)], axis=1) + eye
    pivots = jnp.zeros((NB, 128), F32)
    for j in range(0, NB, STEP):
        c = [jnp.broadcast_to(x[:, j + b : j + b + 1], (NB, 128)) for b in range(STEP)]
        r = [x[j + a : j + a + 1, :] for a in range(STEP)]
        update = None
        for b in range(STEP):
            pivot = c[b][j + b : j + b + 1, :]
            pivots = jnp.where(rows == j + b, pivot, pivots)
            factor = jnp.where(rows > j + b, c[b] * (1.0 / pivot), 0.0)
            for later in range(b + 1, STEP):
                c[later] = c[later] - factor * c[later][j + b : j + b + 1, :]
                r[later] = r[later] - factor[j + later : j + later + 1, :] * r[b]
            term = factor * r[b]
            update = term if update is None else update + term
        x = x - update
    x = x * lax.rsqrt(pivots)
    return x[:, 64 : 64 + NB]


def cholesky_step(m_ref, b):
    n = ROWS
    m = m_ref[...]
    w = small_inverse(m[0:NB, 0:NB])
    col = lax.broadcasted_iota(jnp.int32, (n, n), 1)
    top = dot(w, m[0:NB, :], precision=HIGHEST)
    top = jnp.concatenate([w, top[:, NB:]], axis=1)
    below = dot(m[:, 0:NB], w, ((1,), (1,)), HIGHEST)
    row = lax.broadcasted_iota(jnp.int32, (n, NB), 0)
    below = jnp.where((row >= NB) & (row < n - NB * b), below, 0.0)
    new = jnp.where(col < NB, 0.0, m) - dot(below, top, precision=HIGHEST)
    new = jnp.concatenate([new[NB:], top], axis=0)
    m_ref[...] = jnp.concatenate([new[:, NB:], new[:, :NB]], axis=1)


class Links:
    def __init__(self, send, recv):
        self.send, self.recv, self.used, self.copies = send, recv, 0, []

    def start(self, src, dst, device):
        copy = pltpu.make_async_remote_copy(
            src_ref=src,
            dst_ref=dst,
            send_sem=self.send.at[self.used],
            recv_sem=self.recv.at[self.used],
            device_id=device,
            device_id_type=MESH,
        )
        copy.start()
        self.used += 1
        self.copies.append(copy)
        return copy

    def drain(self):
        for copy in self.copies:
            copy.wait_send()


class RingSum:
    def __init__(self, links, me, to, part, relay, landing):
        self.links, self.me, self.to, self.part = links, me, to, part
        self.relay, self.landing = relay, landing
        self.right, self.left, self.far = (lax.rem(me + d, 4) for d in (1, 3, 2))

    def start(self):
        go = self.links.start
        right, left = self.to(self.right), self.to(self.left)
        self.a = go(self.part(self.far, 0), self.relay.at[0], right)
        self.b = go(self.part(self.far, 1), self.relay.at[1], left)
        self.c = go(self.part(self.right, 1), self.landing.at[0, 1], right)
        self.d = go(self.part(self.left, 0), self.landing.at[1, 0], left)

    def middle(self):
        go = self.links.start
        self.a.wait_recv()
        self.relay[0] = self.relay[0] + self.part(self.right, 0)[...]
        self.e = go(self.relay.at[0], self.landing.at[0, 0], self.to(self.right))
        self.b.wait_recv()
        self.relay[1] = self.relay[1] + self.part(self.left, 1)[...]
        self.f = go(self.relay.at[1], self.landing.at[1, 1], self.to(self.left))

    def finish(self, half):
        for copy in (self.d, self.e) if half == 0 else (self.c, self.f):
            copy.wait_recv()
        return self.part(self.me, half)[...] + (self.landing[0, half] + self.landing[1, half])


class RingGather:
    def __init__(self, links, me, to, part):
        self.links, self.me, self.to, self.part = links, me, to, part
        self.right, self.left = lax.rem(me + 1, 4), lax.rem(me + 3, 4)

    def go(self, place, half, device):
        ref = self.part(place, half)
        return self.links.start(ref, ref, self.to(device))

    def start(self):
        self.a = self.go(self.me, 0, self.right)
        self.b = self.go(self.me, 1, self.left)
        self.c = self.go(self.me, 1, self.right)
        self.d = self.go(self.me, 0, self.left)

    def middle(self):
        self.a.wait_recv()
        self.e = self.go(self.left, 0, self.right)
        self.b.wait_recv()
        self.f = self.go(self.right, 1, self.left)

    def near(self):
        self.c.wait_recv()
        self.d.wait_recv()

    def finish(self):
        self.near()
        self.e.wait_recv()
        self.f.wait_recv()


def exchange_kernel(
    momentum, gradient, right_in, right_out, ortho_out, scale_out,
    mom, grad, rown, comb, rall, summed, relay_b, landing_b, relay_a, landing_a,
    part_left, core_in, tiles, tiles_in, tile_out, left_tiles, left_t,
    gram_y, gram_all, chol, part_t, relay_t, landing_t, t_all, squares,
    send, recv, load, many,
):
    x, f, y = lax.axis_index("rep"), lax.axis_index("fsdp"), lax.axis_index("tp")
    z, core = f // 2, lax.rem(f, 2)
    q = x * 8 + z

    def at(x=x, z=z, core=core, y=y):
        return {"rep": x, "fsdp": z * 2 + core, "tp": y}

    def plane(d):
        other = lax.rem(q + d, 32)
        return other, at(x=other // 8, z=lax.rem(other, 8))

    to_x = lambda p: at(x=p)
    to_y = lambda p: at(y=p)
    partner = at(core=1 - core)
    links = Links(send, recv)

    load_r = pltpu.make_async_copy(right_in, rown, load.at[0])
    load_m = pltpu.make_async_copy(momentum, mom, load.at[1])
    load_g = pltpu.make_async_copy(gradient, grad, load.at[2])
    load_r.start()
    load_m.start()
    load_g.start()

    barrier = pltpu.get_barrier_semaphore()

    def greet(d, carry):
        pl.semaphore_signal(barrier, inc=1, device_id=plane(d)[1], device_id_type=MESH)
        return carry

    for d in (1, 2, 3):
        pl.semaphore_signal(barrier, inc=1, device_id=to_y(lax.rem(y + d, 4)), device_id_type=MESH)
    pl.semaphore_signal(barrier, inc=1, device_id=partner, device_id_type=MESH)
    lax.fori_loop(1, 32, greet, 0)

    load_r.wait()
    for p in range(4):
        rall[p, pl.ds(pl.multiple_of(64 * y, 64), 64), :] = rown[:, CHUNK * p : CHUNK * (p + 1)]
    load_m.wait()
    load_g.wait()
    for p in range(4):
        cols = slice(CHUNK * p, CHUNK * (p + 1))
        comb[p] = mom[:, cols] + grad[:, cols]
    pl.semaphore_wait(barrier, 35)

    def rank_rows(p, h):
        return pl.ds(pl.multiple_of(64 * p + 32 * h, 32), 32)

    def half(h):
        return slice(128 * h, 128 * (h + 1))

    sum_b = RingSum(links, x, to_x, lambda p, h: comb.at[p, half(h), 0:EARLY], relay_b, landing_b)
    gather_b = RingGather(links, y, to_y, lambda p, h: rall.at[x, rank_rows(p, h), 0:EARLY])
    gather_a = RingGather(links, y, to_y, lambda p, h: rall.at[:, rank_rows(p, h), EARLY:CHUNK])
    sum_b.start()
    gather_b.start()
    gather_a.start()
    gather_b.middle()
    sum_b.middle()
    gather_a.middle()
    gather_b.finish()
    gather_a.finish()
    total = None
    for p in range(4):
        term = dot3(comb[p, :, EARLY:CHUNK], rall[p, :, EARLY:CHUNK], ((1,), (1,)))
        total = term if total is None else total + term
    for h in range(2):
        summed[half(h), 0:EARLY] = sum_b.finish(h)
    total = total + dot3(summed[:, 0:EARLY], rall[x, :, 0:EARLY], ((1,), (1,)))
    part_left[0] = total[0:128]
    part_left[1] = total[128:256]

    swap = links.start(part_left.at[1 - core], core_in, partner)
    sum_a = RingSum(links, x, to_x, lambda p, h: comb.at[p, half(h), EARLY:CHUNK], relay_a, landing_a)
    sum_a.start()
    swap.wait_recv()
    mine = part_left[core] + core_in[...]
    tiles[0:16] = mine[:, 0:128].reshape(16, 8, 128)
    tiles[16:32] = mine[:, 128:256].reshape(16, 8, 128)

    def scatter(d, carry):
        other, device = plane(d)
        pltpu.make_async_remote_copy(
            src_ref=tiles.at[other], dst_ref=tiles_in.at[d - 1], send_sem=many.at[0],
            recv_sem=many.at[1], device_id=device, device_id_type=MESH,
        ).start()
        return carry

    def gather(d, carry):
        pltpu.make_async_remote_copy(
            src_ref=tile_out, dst_ref=left_tiles.at[core, q], send_sem=many.at[2],
            recv_sem=many.at[3], device_id=plane(d)[1], device_id_type=MESH,
        ).start()
        return carry

    def wait_many(i, ref):
        pltpu.make_async_copy(ref, ref, many.at[i]).wait()

    lax.fori_loop(1, 32, scatter, 0)
    wait_many(1, tiles_in)
    tile = (tiles[q] + jnp.sum(tiles_in[...], axis=0)) * 0.25
    tile_out[...] = tile
    left_tiles[core, q] = tile
    lax.fori_loop(1, 32, gather, 0)
    sum_a.middle()
    wait_many(3, tiles_in)
    swap = links.start(left_tiles.at[core], left_tiles.at[core], partner)
    for h in range(2):
        summed[half(h), EARLY:CHUNK] = sum_a.finish(h)
    swap.wait_recv()
    left = jnp.concatenate(
        [
            jnp.concatenate([left_tiles[h, 0:16].reshape(128, 128), left_tiles[h, 16:32].reshape(128, 128)], axis=1)
            for h in range(2)
        ],
        axis=0,
    )
    left_t[...] = left.T

    for h in range(2):
        part_t[h] = dot3(left_t[half(h), :], summed[...])

    def y_rows(p, lo=0, n=32):
        return pl.ds(pl.multiple_of(32 * p + lo, n), n)

    sum_t = RingSum(links, y, to_y, lambda p, h: part_t.at[h, y_rows(p)], relay_t, landing_t)
    sum_t.start()
    slab = left_t[pl.ds(pl.multiple_of((core * 4 + x) * 32, 32), 32), :]
    gram_y[y] = dot(slab, left, precision=HIGHEST)
    grams = [links.start(gram_y.at[y], gram_y.at[y], to_y(lax.rem(y + d, 4))) for d in (1, 3, 2)]
    for copy in grams:
        copy.wait_recv()
    gram_all[core, x] = (gram_y[0] + gram_y[1]) + (gram_y[2] + gram_y[3])
    grams = [links.start(gram_all.at[core, x], gram_all.at[core, x], to_x(lax.rem(x + d, 4))) for d in (1, 3, 2)]
    sum_t.middle()
    for copy in grams:
        copy.wait_recv()
    swap = links.start(gram_all.at[core], gram_all.at[core], partner)
    for h in range(2):
        t_all[h, x, y_rows(y), :] = sum_t.finish(h)

    y_first = RingGather(links, y, to_y, lambda p, h: t_all.at[0, x, y_rows(p, 16 * h, 16)])
    x_first = RingGather(links, x, to_x, lambda p, h: t_all.at[1, p, y_rows(y, 16 * h, 16)])
    y_first.start()
    x_first.start()
    swap.wait_recv()
    for c in range(2):
        for p in range(4):
            chol[128 * c + 32 * p : 128 * c + 32 * p + 32, :] = gram_all[c, p]
    y_first.middle()
    x_first.middle()
    cholesky_step(chol, 0)
    y_first.finish()
    x_first.finish()
    then_x = RingGather(links, x, to_x, lambda p, h: t_all.at[0, p, slice(64 * h, 64 * (h + 1))])
    then_y = RingGather(links, y, to_y, lambda p, h: t_all.at[1, :, y_rows(p, 16 * h, 16)])
    then_x.start()
    then_y.start()
    cholesky_step(chol, 1)
    cholesky_step(chol, 2)
    then_x.middle()
    then_y.middle()
    cholesky_step(chol, 3)
    inverse = chol[...]
    ortho_out[...] = dot(left, inverse, ((1,), (1,)), HIGHEST)
    then_x.finish()
    then_y.finish()

    ih, il = split(inverse * 0.25)
    sums = None
    for p in range(4):
        th, tl = split(jnp.concatenate([t_all[0, p], t_all[1, p]], axis=0))
        right = dot(ih, th) + (dot(ih, tl) + dot(il, th))
        right_out[:, CHUNK * p : CHUNK * (p + 1)] = right
        term = jnp.sum(right * right, axis=1, keepdims=True)
        sums = term if sums is None else sums + term
    squares[f] = jnp.broadcast_to(sums, (ROWS, 128)).T[0:8]

    def share(d, carry):
        other = lax.rem(f + d, 16)
        pltpu.make_async_remote_copy(
            src_ref=squares.at[f], dst_ref=squares.at[f], send_sem=many.at[4],
            recv_sem=many.at[5], device_id=at(z=other // 2, core=lax.rem(other, 2)), device_id_type=MESH,
        ).start()
        return carry

    lax.fori_loop(1, 16, share, 0)
    wait_many(5, squares.at[0:15])
    scale_out[...] = lax.rsqrt(jnp.sum(squares[...], axis=0) / TOTAL_COLS + norm_eps)
    wait_many(0, tiles_in)
    wait_many(2, tiles_in)
    wait_many(4, squares.at[0:15])
    links.drain()


def exchange(momentum, gradient, right_t):
    vmem = lambda *shape: pltpu.VMEM(shape, F32)
    return pl.pallas_call(
        exchange_kernel,
        out_shape=(
            jax.ShapeDtypeStruct((ROWS, COLS), F32),
            jax.ShapeDtypeStruct((ROWS, ROWS), F32),
            jax.ShapeDtypeStruct((8, ROWS), F32),
        ),
        in_specs=[pl.BlockSpec(memory_space=pl.ANY)] * 3,
        out_specs=(pl.BlockSpec(memory_space=pltpu.VMEM),) * 3,
        scratch_shapes=[
            vmem(ROWS, COLS),
            vmem(ROWS, COLS),
            vmem(64, COLS),
            vmem(4, ROWS, CHUNK),
            vmem(4, ROWS, CHUNK),
            vmem(ROWS, CHUNK),
            vmem(2, 128, EARLY),
            vmem(2, 2, 128, EARLY),
            vmem(2, 128, LATE),
            vmem(2, 2, 128, LATE),
            vmem(2, 128, ROWS),
            vmem(128, ROWS),
            vmem(32, 8, 128),
            vmem(31, 8, 128),
            vmem(8, 128),
            vmem(2, 32, 8, 128),
            vmem(ROWS, ROWS),
            vmem(4, 32, ROWS),
            vmem(2, 4, 32, ROWS),
            vmem(ROWS, ROWS),
            vmem(2, 128, CHUNK),
            vmem(2, 32, CHUNK),
            vmem(2, 2, 32, CHUNK),
            vmem(2, 4, 128, CHUNK),
            vmem(16, 8, ROWS),
            pltpu.SemaphoreType.DMA((64,)),
            pltpu.SemaphoreType.DMA((64,)),
            pltpu.SemaphoreType.DMA((3,)),
            pltpu.SemaphoreType.DMA((6,)),
        ],
        compiler_params=pltpu.CompilerParams(
            collective_id=0, has_side_effects=True, vmem_limit_bytes=48 * 1024 * 1024
        ),
        cost_estimate=pl.CostEstimate(flops=4 * 2 * ROWS * ROWS * COLS, bytes_accessed=11_000_000, transcendentals=0),
        name="exchange",
    )(momentum, gradient, right_t)


def update_kernel(ortho, scale, right, weights, momentum, gradient, new_weights, new_momentum, new_right):
    start = pl.multiple_of(lax.axis_index("tp") * 64, 64)
    basis = ortho[...]
    value = right[...]
    rh, rl = split(value)
    sh, sl = split(basis * scale[0:1, :])
    update = dot(basis.astype(BF16), rh)
    normal = dot(sh, rh) + (dot(sh, rl) + dot(sl, rh))
    new_momentum[...] = (momentum[...] + gradient[...]) - (1.0 - momentum_decay) * update
    new_weights[...] = weights[...] - learning_rate * normal
    column = jnp.broadcast_to(scale[0:1, :], (128, ROWS)).T
    both = jnp.concatenate([column] * (value.shape[1] // 128), axis=1) * value
    new_right[...] = both[0:64]
    for p in range(1, 4):
        @pl.when(start == 64 * p)
        def _(p=p):
            new_right[...] = both[64 * p : 64 * (p + 1)]


def update(ortho, scale, right, weights, momentum, gradient):
    width = 256
    whole = lambda *shape: pl.BlockSpec(shape, lambda i: (0, 0))
    block = pl.BlockSpec((ROWS, width), lambda i: (0, i))
    return pl.pallas_call(
        update_kernel,
        grid=(COLS // width,),
        out_shape=(
            jax.ShapeDtypeStruct((ROWS, COLS), F32),
            jax.ShapeDtypeStruct((ROWS, COLS), F32),
            jax.ShapeDtypeStruct((64, COLS), F32),
        ),
        in_specs=[whole(ROWS, ROWS), whole(8, ROWS), block, block, block, block],
        out_specs=(block, block, pl.BlockSpec((64, width), lambda i: (0, i))),
        compiler_params=pltpu.CompilerParams(vmem_limit_bytes=32 * 1024 * 1024),
        name="update",
    )(ortho, scale, right, weights, momentum, gradient)


def local(weights, momentum, gradient, right_factor):
    right, ortho, scale = exchange(momentum, gradient, right_factor.T)
    new_weights, new_momentum, new_right_t = update(ortho, scale, right, weights, momentum, gradient)
    return (new_weights, new_momentum, new_right_t.T)


def solution(mesh):
    return jax.shard_map(
        local,
        mesh=mesh,
        in_specs=(
            P("tp", "fsdp"),
            P(("rep", "tp"), "fsdp"),
            P(("rep", "tp"), "fsdp"),
            P("fsdp", "tp"),
        ),
        out_specs=(P("tp", "fsdp"), P(("rep", "tp"), "fsdp"), P("fsdp", "tp")),
        check_vma=False,
    )
```

```python
import functools

import jax
import jax.numpy as jnp
from jax import lax
from jax.experimental import pallas as pl
from jax.experimental.pallas import tpu as pltpu
from jax.sharding import PartitionSpec as P

MESH = pl.DeviceIdType.MESH
HIGHEST = lax.Precision.HIGHEST
F32 = jnp.float32
BF16 = jnp.bfloat16

momentum_decay = 0.95
learning_rate = 0.05
norm_eps = 1e-06

ROWS = 256
COLS = 3328
CHUNK = 832
EARLY = 512
LATE = CHUNK - EARLY
EARLY_COLS = 4 * EARLY
LATE_COLS = 4 * LATE
TOTAL_COLS = 53248
NB = 64
STEP = 8


def dot(a, b, dims=((1,), (0,)), precision=None):
    return lax.dot_general(a, b, (dims, ((), ())), precision=precision, preferred_element_type=F32)


def split(a):
    high = a.astype(BF16)
    return high, (a - high.astype(F32)).astype(BF16)


def dot3(a, b, dims=((1,), (0,))):
    ah, al = split(a)
    bh, bl = split(b)
    return dot(ah, bh, dims) + (dot(ah, bl, dims) + dot(al, bh, dims))


def cholesky_pieces(m_ref, x_ref, pivots_ref):
    n = ROWS
    rows = lax.broadcasted_iota(jnp.int32, (NB, 128), 0)
    cols = lax.broadcasted_iota(jnp.int32, (NB, 128), 1)
    eye = jnp.where(cols == rows + 64, 1.0, 0.0).astype(F32)

    def pivots_from(j):
        if j == 0:
            x_ref[...] = jnp.concatenate([m_ref[0:NB, 0:NB], jnp.zeros((NB, 128 - NB), F32)], axis=1) + eye
        x = x_ref[...]
        pivots = pivots_ref[...]
        c = [jnp.broadcast_to(x[:, j + b : j + b + 1], (NB, 128)) for b in range(STEP)]
        r = [x[j + a : j + a + 1, :] for a in range(STEP)]
        update = None
        for b in range(STEP):
            pivot = c[b][j + b : j + b + 1, :]
            pivots = jnp.where(rows == j + b, pivot, pivots)
            factor = jnp.where(rows > j + b, c[b] * (1.0 / pivot), 0.0)
            for later in range(b + 1, STEP):
                c[later] = c[later] - factor * c[later][j + b : j + b + 1, :]
                r[later] = r[later] - factor[j + later : j + later + 1, :] * r[b]
            term = factor * r[b]
            update = term if update is None else update + term
        x_ref[...] = x - update
        pivots_ref[...] = pivots

    def rest(block):
        w = (x_ref[...] * lax.rsqrt(pivots_ref[...]))[:, 64 : 64 + NB]
        m = m_ref[...]
        col = lax.broadcasted_iota(jnp.int32, (n, n), 1)
        top = dot(w, m[0:NB, :], precision=HIGHEST)
        top = jnp.concatenate([w, top[:, NB:]], axis=1)
        below = dot(m[:, 0:NB], w, ((1,), (1,)), HIGHEST)
        row = lax.broadcasted_iota(jnp.int32, (n, NB), 0)
        below = jnp.where((row >= NB) & (row < n - NB * block), below, 0.0)
        new = jnp.where(col < NB, 0.0, m) - dot(below, top, precision=HIGHEST)
        new = jnp.concatenate([new[NB:], top], axis=0)
        m_ref[...] = jnp.concatenate([new[:, NB:], new[:, :NB]], axis=1)

    pieces = []
    for block in range(n // NB):
        pieces += [functools.partial(pivots_from, j) for j in range(0, NB, STEP)]
        pieces.append(functools.partial(rest, block))
    return pieces


class Links:
    def __init__(self, send, recv):
        self.send, self.recv, self.used, self.copies = send, recv, 0, []

    def start(self, src, dst, device):
        copy = pltpu.make_async_remote_copy(
            src_ref=src,
            dst_ref=dst,
            send_sem=self.send.at[self.used],
            recv_sem=self.recv.at[self.used],
            device_id=device,
            device_id_type=MESH,
        )
        copy.start()
        self.used += 1
        self.copies.append(copy)
        return copy

    def drain(self):
        for copy in self.copies:
            copy.wait_send()


class RingSum:
    def __init__(self, links, me, to, part, relay, landing):
        self.links, self.me, self.to, self.part = links, me, to, part
        self.relay, self.landing = relay, landing
        self.right, self.left, self.far = (lax.rem(me + d, 4) for d in (1, 3, 2))

    def start(self):
        go = self.links.start
        right, left = self.to(self.right), self.to(self.left)
        self.a = go(self.part(self.far, 0), self.relay.at[0], right)
        self.b = go(self.part(self.far, 1), self.relay.at[1], left)
        self.c = go(self.part(self.right, 1), self.landing.at[0, 1], right)
        self.d = go(self.part(self.left, 0), self.landing.at[1, 0], left)

    def middle(self):
        go = self.links.start
        self.a.wait_recv()
        self.relay[0] = self.relay[0] + self.part(self.right, 0)[...]
        self.e = go(self.relay.at[0], self.landing.at[0, 0], self.to(self.right))
        self.b.wait_recv()
        self.relay[1] = self.relay[1] + self.part(self.left, 1)[...]
        self.f = go(self.relay.at[1], self.landing.at[1, 1], self.to(self.left))

    def finish(self, half):
        for copy in (self.d, self.e) if half == 0 else (self.c, self.f):
            copy.wait_recv()
        return self.part(self.me, half)[...] + (self.landing[0, half] + self.landing[1, half])


class RingGather:
    def __init__(self, links, me, to, part):
        self.links, self.me, self.to, self.part = links, me, to, part
        self.right, self.left = lax.rem(me + 1, 4), lax.rem(me + 3, 4)

    def go(self, place, half, device):
        ref = self.part(place, half)
        return self.links.start(ref, ref, self.to(device))

    def start(self):
        self.a = self.go(self.me, 0, self.right)
        self.b = self.go(self.me, 1, self.left)
        self.c = self.go(self.me, 1, self.right)
        self.d = self.go(self.me, 0, self.left)

    def middle(self):
        self.a.wait_recv()
        self.e = self.go(self.left, 0, self.right)
        self.b.wait_recv()
        self.f = self.go(self.right, 1, self.left)

    def near(self):
        self.c.wait_recv()
        self.d.wait_recv()

    def finish(self):
        self.near()
        self.e.wait_recv()
        self.f.wait_recv()


def exchange_kernel(
    momentum, gradient, right_in, right_out, ortho_out, scale_out, momentum_out,
    early, early_g, late_c, late_g, late, rown, rearly, rlate, summed, relay_b, landing_b, relay_a, landing_a,
    part_left, core_in, tiles, tiles_in, tile_out, left_tiles, left_t,
    gram_y, gram_all, chol, chol_x, chol_pivots, part_a, relay_ta, landing_ta, all_a,
    part_b, relay_tb, landing_tb, all_b, squares,
    send, recv, load, many,
):
    x, f, y = lax.axis_index("rep"), lax.axis_index("fsdp"), lax.axis_index("tp")
    z, core = f // 2, lax.rem(f, 2)
    q = x * 8 + z

    def at(x=x, z=z, core=core, y=y):
        return {"rep": x, "fsdp": z * 2 + core, "tp": y}

    def middle_out(i):
        return ((i + 1) // 2) * (1 - 2 * lax.rem(i, 2))

    def plane(i):
        there_x = lax.rem(x + 2 + middle_out(lax.rem(i, 4)), 4)
        there_z = lax.rem(z + 4 + middle_out(i // 4), 8)
        return there_x * 8 + there_z, at(x=there_x, z=there_z)

    to_x = lambda p: at(x=p)
    to_y = lambda p: at(y=p)
    partner = at(core=1 - core)
    links = Links(send, recv)

    load_r = pltpu.make_async_copy(right_in, rown, load.at[0])
    load_r.start()
    loads = []
    for p in range(4):
        cols = slice(EARLY * p, EARLY * (p + 1))
        loads.append(
            (
                pltpu.make_async_copy(momentum.at[:, cols], early.at[p], load.at[1 + 2 * p]),
                pltpu.make_async_copy(gradient.at[:, cols], early_g.at[p], load.at[2 + 2 * p]),
            )
        )
    loads.append(
        (
            pltpu.make_async_copy(momentum.at[:, EARLY_COLS:COLS], late_c, load.at[9]),
            pltpu.make_async_copy(gradient.at[:, EARLY_COLS:COLS], late_g, load.at[10]),
        )
    )
    for pair in loads:
        for copy in pair:
            copy.start()

    barrier = pltpu.get_barrier_semaphore()

    def greet(d, carry):
        pl.semaphore_signal(barrier, inc=1, device_id=plane(d)[1], device_id_type=MESH)
        return carry

    for d in (1, 2, 3):
        pl.semaphore_signal(barrier, inc=1, device_id=to_y(lax.rem(y + d, 4)), device_id_type=MESH)
    pl.semaphore_signal(barrier, inc=1, device_id=partner, device_id_type=MESH)
    lax.fori_loop(0, 31, greet, 0)

    my_ranks = pl.ds(pl.multiple_of(64 * y, 64), 64)
    load_r.wait()
    rearly[my_ranks, :] = rown[:, pl.ds(pl.multiple_of(EARLY * x, EARLY), EARLY)]
    rlate[my_ranks, :] = rown[:, EARLY_COLS:COLS]
    for p in range(4):
        for copy in loads[p]:
            copy.wait()
        early[p] = early[p] + early_g[p]
    pl.semaphore_wait(barrier, 35)

    def rank_rows(p, h):
        return pl.ds(pl.multiple_of(64 * p + 32 * h, 32), 32)

    def half(h):
        return slice(128 * h, 128 * (h + 1))

    sum_b = RingSum(links, x, to_x, lambda p, h: early.at[p, half(h)], relay_b, landing_b)
    gather_a = RingGather(links, y, to_y, lambda p, h: rlate.at[rank_rows(p, h)])
    gather_b = RingGather(links, y, to_y, lambda p, h: rearly.at[rank_rows(p, h)])
    sum_b.start()
    gather_a.start()
    gather_b.start()
    for copy in loads[4]:
        copy.wait()
    late_c[...] = late_c[...] + late_g[...]
    for p in range(4):
        late[p] = late_c[:, LATE * p : LATE * (p + 1)]
    gather_a.middle()
    sum_b.middle()
    gather_b.middle()
    gather_a.finish()
    total = dot3(late_c[...], rlate[...], ((1,), (1,)))
    gather_b.finish()
    for h in range(2):
        summed[half(h), 0:EARLY] = sum_b.finish(h)
    total = total + dot3(summed[:, 0:EARLY], rearly[...], ((1,), (1,)))
    part_left[0] = total[0:128]
    part_left[1] = total[128:256]

    swap = links.start(part_left.at[1 - core], core_in, partner)
    sum_a = RingSum(links, x, to_x, lambda p, h: late.at[p, half(h)], relay_a, landing_a)
    sum_a.start()
    swap.wait_recv()
    mine = part_left[core] + core_in[...]
    tiles[0:16] = mine[:, 0:128].reshape(16, 8, 128)
    tiles[16:32] = mine[:, 128:256].reshape(16, 8, 128)

    def scatter(d, carry):
        other, device = plane(d)
        pltpu.make_async_remote_copy(
            src_ref=tiles.at[other], dst_ref=tiles_in.at[d], send_sem=many.at[0],
            recv_sem=many.at[1], device_id=device, device_id_type=MESH,
        ).start()
        return carry

    def gather(d, carry):
        pltpu.make_async_remote_copy(
            src_ref=tile_out, dst_ref=left_tiles.at[core, q], send_sem=many.at[2],
            recv_sem=many.at[3], device_id=plane(d)[1], device_id_type=MESH,
        ).start()
        return carry

    def wait_many(i, ref):
        pltpu.make_async_copy(ref, ref, many.at[i]).wait()

    lax.fori_loop(0, 31, scatter, 0)
    wait_many(1, tiles_in)
    tile = (tiles[q] + jnp.sum(tiles_in[...], axis=0)) * 0.25
    tile_out[...] = tile
    left_tiles[core, q] = tile
    lax.fori_loop(0, 31, gather, 0)
    sum_a.middle()
    wait_many(3, tiles_in)
    swap = links.start(left_tiles.at[core], left_tiles.at[core], partner)
    for h in range(2):
        summed[half(h), EARLY:CHUNK] = sum_a.finish(h)
    swap.wait_recv()
    left = jnp.concatenate(
        [
            jnp.concatenate([left_tiles[h, 0:16].reshape(128, 128), left_tiles[h, 16:32].reshape(128, 128)], axis=1)
            for h in range(2)
        ],
        axis=0,
    )
    left_t[...] = left.T

    def y_rows(p, lo=0, n=32):
        return pl.ds(pl.multiple_of(32 * p + lo, n), n)

    class Product:
        def __init__(self, cols, part, relay, landing, whole):
            self.cols, self.part, self.whole = cols, part, whole
            self.sum = RingSum(links, y, to_y, lambda p, h: part.at[h, y_rows(p)], relay, landing)

        def multiply(self):
            for h in range(2):
                self.part[h] = dot3(left_t[half(h), :], summed[:, self.cols])

        def share(self):
            whole = self.whole
            self.first = (
                RingGather(links, y, to_y, lambda p, h: whole.at[0, x, y_rows(p, 16 * h, 16)]),
                RingGather(links, x, to_x, lambda p, h: whole.at[1, p, y_rows(y, 16 * h, 16)]),
            )
            for h in range(2):
                whole[h, x, y_rows(y), :] = self.sum.finish(h)
                self.first[h].start()

        def share_on(self):
            whole = self.whole
            for ring in self.first:
                ring.finish()
            self.then = (
                RingGather(links, x, to_x, lambda p, h: whole.at[0, p, slice(64 * h, 64 * (h + 1))]),
                RingGather(links, y, to_y, lambda p, h: whole.at[1, :, y_rows(p, 16 * h, 16)]),
            )

        def each(self, rings, step):
            for ring in rings:
                getattr(ring, step)()

    a = Product(slice(0, EARLY), part_a, relay_ta, landing_ta, all_a)
    b = Product(slice(EARLY, CHUNK), part_b, relay_tb, landing_tb, all_b)
    a.multiply()
    a.sum.start()
    b.multiply()
    slab = left_t[pl.ds(pl.multiple_of((core * 4 + x) * 32, 32), 32), :]
    gram_y[y] = dot(slab, left, precision=HIGHEST)
    grams = [links.start(gram_y.at[y], gram_y.at[y], to_y(lax.rem(y + d, 4))) for d in (2, 1, 3)]
    a.sum.middle()
    b.sum.start()
    for copy in grams:
        copy.wait_recv()
    gram_all[core, x] = (gram_y[0] + gram_y[1]) + (gram_y[2] + gram_y[3])
    grams = [links.start(gram_all.at[core, x], gram_all.at[core, x], to_x(lax.rem(x + d, 4))) for d in (2, 1, 3)]
    b.sum.middle()
    a.share()
    for copy in grams:
        copy.wait_recv()
    swap = links.start(gram_all.at[core], gram_all.at[core], partner)
    a.each(a.first, "middle")
    b.share()
    swap.wait_recv()
    for c in range(2):
        for p in range(4):
            chol[128 * c + 32 * p : 128 * c + 32 * p + 32, :] = gram_all[c, p]
    pieces = cholesky_pieces(chol, chol_x, chol_pivots)
    once = jnp.minimum(x + 1, 1)

    def work(n):
        now = [pieces.pop(0) for _ in range(n)]

        def step(i, carry):
            for piece in now:
                piece()
            return carry

        lax.fori_loop(0, once, step, 0)

    a.share_on()
    a.each(a.then, "start")
    work(3)
    b.each(b.first, "middle")
    work(8)
    b.share_on()
    a.each(a.then, "middle")
    b.each(b.then, "start")
    work(17)
    b.each(b.then, "middle")
    work(len(pieces))
    inverse = chol[...]
    ortho = dot(left, inverse, ((1,), (1,)), HIGHEST)
    ortho_out[...] = ortho

    ih, il = split(inverse * 0.25)
    sums = jnp.zeros((ROWS, 1), F32)
    for product, first, width in ((a, 0, EARLY), (b, EARLY_COLS, LATE)):
        product.each(product.then, "finish")
        for p in range(4):
            th, tl = split(jnp.concatenate([product.whole[0, p], product.whole[1, p]], axis=0))
            right = dot(ih, th) + (dot(ih, tl) + dot(il, th))
            right_out[:, first + width * p : first + width * (p + 1)] = right
            sums = sums + jnp.sum(right * right, axis=1, keepdims=True)
    squares[f] = jnp.broadcast_to(sums, (ROWS, 128)).T[0:8]

    def share(i, carry):
        there = at(z=lax.rem(z + 4 + middle_out(i // 2), 8), core=lax.rem(core + 1 + i, 2))
        pltpu.make_async_remote_copy(
            src_ref=squares.at[f], dst_ref=squares.at[f], send_sem=many.at[4],
            recv_sem=many.at[5], device_id=there, device_id_type=MESH,
        ).start()
        return carry

    lax.fori_loop(0, 15, share, 0)
    basis = ortho.astype(BF16)
    rate = 1.0 - momentum_decay
    for p in range(4):
        cols = slice(EARLY * p, EARLY * (p + 1))
        momentum_out[:, cols] = early[p] - rate * dot(basis, right_out[:, cols].astype(BF16))
    cols = slice(EARLY_COLS, COLS)
    momentum_out[:, cols] = late_c[...] - rate * dot(basis, right_out[:, cols].astype(BF16))
    wait_many(5, squares.at[0:15])
    scale_out[...] = lax.rsqrt(jnp.sum(squares[...], axis=0) / TOTAL_COLS + norm_eps)
    wait_many(0, tiles_in)
    wait_many(2, tiles_in)
    wait_many(4, squares.at[0:15])
    links.drain()


def exchange(momentum, gradient, right_t):
    vmem = lambda *shape: pltpu.VMEM(shape, F32)
    return pl.pallas_call(
        exchange_kernel,
        out_shape=(
            jax.ShapeDtypeStruct((ROWS, COLS), F32),
            jax.ShapeDtypeStruct((ROWS, ROWS), F32),
            jax.ShapeDtypeStruct((8, ROWS), F32),
            jax.ShapeDtypeStruct((ROWS, COLS), F32),
        ),
        in_specs=[pl.BlockSpec(memory_space=pltpu.HBM)] * 3,
        out_specs=(pl.BlockSpec(memory_space=pltpu.VMEM),) * 4,
        scratch_shapes=[
            vmem(4, ROWS, EARLY),
            vmem(4, ROWS, EARLY),
            vmem(ROWS, LATE_COLS),
            vmem(ROWS, LATE_COLS),
            vmem(4, ROWS, LATE),
            vmem(64, COLS),
            vmem(ROWS, EARLY),
            vmem(ROWS, LATE_COLS),
            vmem(ROWS, CHUNK),
            vmem(2, 128, EARLY),
            vmem(2, 2, 128, EARLY),
            vmem(2, 128, LATE),
            vmem(2, 2, 128, LATE),
            vmem(2, 128, ROWS),
            vmem(128, ROWS),
            vmem(32, 8, 128),
            vmem(31, 8, 128),
            vmem(8, 128),
            vmem(2, 32, 8, 128),
            vmem(ROWS, ROWS),
            vmem(4, 32, ROWS),
            vmem(2, 4, 32, ROWS),
            vmem(ROWS, ROWS),
            vmem(NB, 128),
            vmem(NB, 128),
            vmem(2, 128, EARLY),
            vmem(2, 32, EARLY),
            vmem(2, 2, 32, EARLY),
            vmem(2, 4, 128, EARLY),
            vmem(2, 128, LATE),
            vmem(2, 32, LATE),
            vmem(2, 2, 32, LATE),
            vmem(2, 4, 128, LATE),
            vmem(16, 8, ROWS),
            pltpu.SemaphoreType.DMA((128,)),
            pltpu.SemaphoreType.DMA((128,)),
            pltpu.SemaphoreType.DMA((11,)),
            pltpu.SemaphoreType.DMA((6,)),
        ],
        compiler_params=pltpu.CompilerParams(
            collective_id=0, has_side_effects=True, vmem_limit_bytes=45 * 1024 * 1024
        ),
        cost_estimate=pl.CostEstimate(flops=4 * 2 * ROWS * ROWS * COLS, bytes_accessed=11_000_000, transcendentals=0),
        name="exchange",
    )(momentum, gradient, right_t)


def update_kernel(
    ortho, scale, right, weights, momentum, new_weights, new_momentum, new_right, staged_w, column_ref, staged_r, sems
):
    copies = [pltpu.make_async_copy(momentum, new_momentum, sems.at[0])]
    copies[0].start()
    own = pl.ds(pl.multiple_of(lax.axis_index("tp") * 64, 64), 64)
    sh, sl = split(ortho[...] * scale[0:1, :])
    column_ref[...] = jnp.broadcast_to(scale[0:1, :], (128, ROWS)).T
    column = column_ref[own, :]
    column = jnp.concatenate([column] * (WIDTH // 128), axis=1)
    for i in range(COLS // WIDTH):
        cols = slice(WIDTH * i, WIDTH * (i + 1))
        rh, rl = split(right[:, cols])
        normal = dot(sh, rh) + (dot(sh, rl) + dot(sl, rh))
        staged_w[:, cols] = weights[:, cols] - learning_rate * normal
        staged_r[:, cols] = column * right[own, cols]
        copies.append(pltpu.make_async_copy(staged_w.at[:, cols], new_weights.at[:, cols], sems.at[2 * i + 1]))
        copies[-1].start()
        copies.append(
            pltpu.make_async_copy(staged_r.at[:, cols], new_right.at[:, cols], sems.at[2 * i + 2])
        )
        copies[-1].start()
    for copy in copies:
        copy.wait()


WIDTH = 1664


def update(ortho, scale, right, weights, momentum):
    return pl.pallas_call(
        update_kernel,
        out_shape=(
            jax.ShapeDtypeStruct((ROWS, COLS), F32),
            jax.ShapeDtypeStruct((ROWS, COLS), F32),
            jax.ShapeDtypeStruct((64, COLS), F32),
        ),
        in_specs=[pl.BlockSpec(memory_space=pltpu.VMEM)] * 5,
        out_specs=(pl.BlockSpec(memory_space=pltpu.HBM),) * 3,
        scratch_shapes=[
            pltpu.VMEM((ROWS, COLS), F32),
            pltpu.VMEM((ROWS, 128), F32),
            pltpu.VMEM((64, COLS), F32),
            pltpu.SemaphoreType.DMA((2 * (COLS // WIDTH) + 1,)),
        ],
        compiler_params=pltpu.CompilerParams(vmem_limit_bytes=40 * 1024 * 1024),
        name="update",
    )(ortho, scale, right, weights, momentum)


def local(weights, momentum, gradient, right_factor):
    right, ortho, scale, moved = exchange(momentum, gradient, right_factor.T)
    new_weights, new_momentum, new_right_t = update(ortho, scale, right, weights, moved)
    return (new_weights, new_momentum, new_right_t.T)


def solution(mesh):
    return jax.shard_map(
        local,
        mesh=mesh,
        in_specs=(
            P("tp", "fsdp"),
            P(("rep", "tp"), "fsdp"),
            P(("rep", "tp"), "fsdp"),
            P("fsdp", "tp"),
        ),
        out_specs=(P("tp", "fsdp"), P(("rep", "tp"), "fsdp"), P("fsdp", "tp")),
        check_vma=False,
    )
```

```python
import functools

import jax
import jax.numpy as jnp
from jax import lax
from jax.experimental import pallas as pl
from jax.experimental.pallas import tpu as pltpu
from jax.sharding import PartitionSpec as P

MESH = pl.DeviceIdType.MESH
HIGHEST = lax.Precision.HIGHEST
F32 = jnp.float32
BF16 = jnp.bfloat16

momentum_decay = 0.95
learning_rate = 0.05
norm_eps = 1e-06

ROWS = 256
COLS = 3328
CHUNK = 832
EARLY = 512
LATE = CHUNK - EARLY
EARLY_COLS = 4 * EARLY
LATE_COLS = 4 * LATE
TOTAL_COLS = 53248
SHARES = (40, 24)
SENDS, ARRIVALS = 19, 53
NB = 64
STEP = 8


def dot(a, b, dims=((1,), (0,)), precision=None):
    return lax.dot_general(a, b, (dims, ((), ())), precision=precision, preferred_element_type=F32)


def split(a):
    high = a.astype(BF16)
    return high, (a - high.astype(F32)).astype(BF16)


def dot3(a, b, dims=((1,), (0,))):
    ah, al = split(a)
    bh, bl = split(b)
    return dot(ah, bh, dims) + (dot(ah, bl, dims) + dot(al, bh, dims))


def cholesky_pieces(m_ref, x_ref, pivots_ref):
    n = ROWS
    rows = lax.broadcasted_iota(jnp.int32, (NB, 128), 0)
    cols = lax.broadcasted_iota(jnp.int32, (NB, 128), 1)
    eye = jnp.where(cols == rows + 64, 1.0, 0.0).astype(F32)

    def pivots_from(j):
        if j == 0:
            x_ref[...] = jnp.concatenate([m_ref[0:NB, 0:NB], jnp.zeros((NB, 128 - NB), F32)], axis=1) + eye
        x = x_ref[...]
        pivots = pivots_ref[...]
        c = [jnp.broadcast_to(x[:, j + b : j + b + 1], (NB, 128)) for b in range(STEP)]
        r = [x[j + a : j + a + 1, :] for a in range(STEP)]
        update = None
        for b in range(STEP):
            pivot = c[b][j + b : j + b + 1, :]
            pivots = jnp.where(rows == j + b, pivot, pivots)
            factor = jnp.where(rows > j + b, c[b] * (1.0 / pivot), 0.0)
            for later in range(b + 1, STEP):
                c[later] = c[later] - factor * c[later][j + b : j + b + 1, :]
                r[later] = r[later] - factor[j + later : j + later + 1, :] * r[b]
            term = factor * r[b]
            update = term if update is None else update + term
        x_ref[...] = x - update
        pivots_ref[...] = pivots

    def rest(block):
        w = (x_ref[...] * lax.rsqrt(pivots_ref[...]))[:, 64 : 64 + NB]
        m = m_ref[...]
        col = lax.broadcasted_iota(jnp.int32, (n, n), 1)
        top = dot(w, m[0:NB, :], precision=HIGHEST)
        top = jnp.concatenate([w, top[:, NB:]], axis=1)
        below = dot(m[:, 0:NB], w, ((1,), (1,)), HIGHEST)
        row = lax.broadcasted_iota(jnp.int32, (n, NB), 0)
        below = jnp.where((row >= NB) & (row < n - NB * block), below, 0.0)
        new = jnp.where(col < NB, 0.0, m) - dot(below, top, precision=HIGHEST)
        new = jnp.concatenate([new[NB:], top], axis=0)
        m_ref[...] = jnp.concatenate([new[:, NB:], new[:, :NB]], axis=1)

    pieces = []
    for block in range(n // NB):
        pieces += [functools.partial(pivots_from, j) for j in range(0, NB, STEP)]
        pieces.append(functools.partial(rest, block))
    return pieces


class Links:
    def __init__(self, send, recv):
        self.send, self.recv, self.sends, self.recvs, self.at_end = send, recv, 0, 0, []

    def wait(self, sem, ref):
        pltpu.make_async_copy(ref, ref, sem).wait()

    def group(self, ref):
        sem = self.send.at[self.sends]
        self.sends += 1
        self.at_end.append(lambda: self.wait(sem, ref))
        return sem

    def arrivals(self):
        sem = self.recv.at[self.recvs]
        self.recvs += 1
        return sem

    def start(self, src, dst, device, group=None, arrivals=None):
        alone = group is None
        if alone:
            group = self.send.at[self.sends]
            self.sends += 1
        copy = pltpu.make_async_remote_copy(
            src_ref=src,
            dst_ref=dst,
            send_sem=group,
            recv_sem=self.arrivals() if arrivals is None else arrivals,
            device_id=device,
            device_id_type=MESH,
        )
        copy.start()
        if alone:
            self.at_end.append(copy.wait_send)
        return copy

    def drain(self):
        for wait in self.at_end:
            wait()


class RingSum:
    def __init__(self, links, me, to, part, relay, landing, sent):
        self.links, self.me, self.to, self.part = links, me, to, part
        self.relay, self.landing = relay, landing
        self.right, self.left, self.far = (lax.rem(me + d, 4) for d in (1, 3, 2))
        self.group = links.group(sent)

    def go(self, src, dst, place):
        return self.links.start(src, dst, self.to(place), self.group)

    def start(self):
        self.start_far()
        self.start_near()

    def start_far(self):
        self.a = self.go(self.part(self.far, 0), self.relay(0), self.right)
        self.b = self.go(self.part(self.far, 1), self.relay(1), self.left)

    def start_near(self):
        self.c = self.go(self.part(self.right, 1), self.landing(0, 1), self.right)
        self.d = self.go(self.part(self.left, 0), self.landing(1, 0), self.left)

    def middle(self):
        self.a.wait_recv()
        ref = self.relay(0)
        ref[...] = ref[...] + self.part(self.right, 0)[...]
        self.e = self.go(ref, self.landing(0, 0), self.right)
        self.b.wait_recv()
        ref = self.relay(1)
        ref[...] = ref[...] + self.part(self.left, 1)[...]
        self.f = self.go(ref, self.landing(1, 1), self.left)

    def finish(self, half):
        for copy in (self.d, self.e) if half == 0 else (self.c, self.f):
            copy.wait_recv()
        return self.part(self.me, half)[...] + (self.landing(0, half)[...] + self.landing(1, half)[...])


class RingGather:
    def __init__(self, links, me, to, part, group, first, rest):
        self.links, self.me, self.to, self.part = links, me, to, part
        self.group, self.first, self.rest = group, first, rest
        self.right, self.left = lax.rem(me + 1, 4), lax.rem(me + 3, 4)

    def go(self, place, half, device, arrivals):
        ref = self.part(place, half)
        self.links.start(ref, ref, self.to(device), self.group, arrivals)

    def start(self):
        self.go(self.me, 0, self.right, self.first)
        self.go(self.me, 1, self.left, self.first)
        self.go(self.me, 1, self.right, self.rest)
        self.go(self.me, 0, self.left, self.rest)

    def forward(self):
        self.go(self.left, 0, self.right, self.rest)
        self.go(self.right, 1, self.left, self.rest)


def exchange_kernel(
    momentum, gradient, right_in, right_out, ortho_out, scale_out, momentum_out,
    early, early_g, late_c, late_g, late, rown, rearly, rlate, summed, relay_b, landing_b, relay_a, landing_a,
    part_left, core_in, tiles, tiles_in, tile_out, left_tiles, left_t,
    gram_y, gram_all, chol, chol_x, chol_pivots, part_a, relay_ta, landing_ta, all_a,
    part_b, relay_tb, landing_tb, all_b, squares,
    send, recv, load, many,
):
    x, f, y = lax.axis_index("rep"), lax.axis_index("fsdp"), lax.axis_index("tp")
    z, core = f // 2, lax.rem(f, 2)
    q = x * 8 + z

    def at(x=x, z=z, core=core, y=y):
        return {"rep": x, "fsdp": z * 2 + core, "tp": y}

    def middle_out(i):
        return ((i + 1) // 2) * (1 - 2 * lax.rem(i, 2))

    def plane(i):
        there_x = lax.rem(x + 2 + middle_out(lax.rem(i, 4)), 4)
        there_z = lax.rem(z + 4 + middle_out(i // 4), 8)
        return there_x * 8 + there_z, at(x=there_x, z=there_z)

    to_x = lambda p: at(x=p)
    to_y = lambda p: at(y=p)
    partner = at(core=1 - core)
    links = Links(send, recv)

    load_r = pltpu.make_async_copy(right_in, rown, load.at[0])
    load_r.start()
    order = [lax.rem(x + d, 4) for d in (2, 1, 3, 0)]
    loads = []
    for i, p in enumerate(order):
        cols = pl.ds(pl.multiple_of(EARLY * p, EARLY), EARLY)
        loads.append(
            (
                pltpu.make_async_copy(momentum.at[:, cols], early.at[p], load.at[1 + 2 * i]),
                pltpu.make_async_copy(gradient.at[:, cols], early_g.at[p], load.at[2 + 2 * i]),
            )
        )
    loads.append(
        (
            pltpu.make_async_copy(momentum.at[:, EARLY_COLS:COLS], late_c, load.at[9]),
            pltpu.make_async_copy(gradient.at[:, EARLY_COLS:COLS], late_g, load.at[10]),
        )
    )
    for pair in loads[:4]:
        for copy in pair:
            copy.start()

    def loaded(i):
        for copy in loads[i]:
            copy.wait()
        early[order[i]] = early[order[i]] + early_g[order[i]]

    barrier = pltpu.get_barrier_semaphore()

    def greet(d, carry):
        pl.semaphore_signal(barrier, inc=1, device_id=plane(d)[1], device_id_type=MESH)
        return carry

    for d in (1, 2, 3):
        pl.semaphore_signal(barrier, inc=1, device_id=to_y(lax.rem(y + d, 4)), device_id_type=MESH)
    pl.semaphore_signal(barrier, inc=1, device_id=partner, device_id_type=MESH)
    lax.fori_loop(0, 31, greet, 0)

    my_ranks = pl.ds(pl.multiple_of(64 * y, 64), 64)
    load_r.wait()
    rearly[my_ranks, :] = rown[:, pl.ds(pl.multiple_of(EARLY * x, EARLY), EARLY)]
    rlate[my_ranks, :] = rown[:, EARLY_COLS:COLS]
    loaded(0)
    pl.semaphore_wait(barrier, 35)

    def rank_rows(p, h):
        return pl.ds(pl.multiple_of(64 * p + 32 * h, 32), 32)

    def half(h):
        return slice(128 * h, 128 * (h + 1))

    sum_b = RingSum(
        links, x, to_x, lambda p, h: early.at[p, half(h)],
        lambda h: relay_b.at[h], lambda i, h: landing_b.at[i, h], early.at[0:3],
    )
    gathers = []
    for ref in (rlate, rearly):
        sems = (links.group(ref.at[0:192]), links.arrivals(), links.arrivals())
        gathers.append(RingGather(links, y, to_y, lambda p, h, ref=ref: ref.at[rank_rows(p, h)], *sems))
    gather_a, gather_b = gathers
    sum_b.start_far()
    gather_a.start()
    gather_b.start()
    loaded(1)
    loaded(2)
    sum_b.start_near()
    for copy in loads[4]:
        copy.start()
    loaded(3)
    for copy in loads[4]:
        copy.wait()
    late_c[...] = late_c[...] + late_g[...]
    for p in range(4):
        late[p] = late_c[:, LATE * p : LATE * (p + 1)]
    links.wait(gather_a.first, rlate.at[0:64])
    gather_a.forward()
    sum_b.middle()
    links.wait(gather_b.first, rearly.at[0:64])
    gather_b.forward()
    links.wait(gather_a.rest, rlate.at[0:128])
    total = dot3(late_c[...], rlate[...], ((1,), (1,)))
    links.wait(gather_b.rest, rearly.at[0:128])
    for h in range(2):
        summed[half(h), 0:EARLY] = sum_b.finish(h)
    total = total + dot3(summed[:, 0:EARLY], rearly[...], ((1,), (1,)))
    part_left[0] = total[0:128]
    part_left[1] = total[128:256]

    swap = links.start(part_left.at[1 - core], core_in, partner)
    sum_a = RingSum(
        links, x, to_x, lambda p, h: late.at[p, half(h)],
        lambda h: relay_a.at[h], lambda i, h: landing_a.at[i, h], late.at[0:3],
    )
    swap.wait_recv()
    mine = part_left[core] + core_in[...]
    tiles[0:16] = mine[:, 0:128].reshape(16, 8, 128)
    tiles[16:32] = mine[:, 128:256].reshape(16, 8, 128)

    def scatter(d, carry):
        other, device = plane(d)
        pltpu.make_async_remote_copy(
            src_ref=tiles.at[other], dst_ref=tiles_in.at[d], send_sem=many.at[0],
            recv_sem=many.at[1], device_id=device, device_id_type=MESH,
        ).start()
        return carry

    def gather(d, carry):
        pltpu.make_async_remote_copy(
            src_ref=tile_out, dst_ref=left_tiles.at[core, q], send_sem=many.at[2],
            recv_sem=many.at[3], device_id=plane(d)[1], device_id_type=MESH,
        ).start()
        return carry

    def wait_many(i, ref):
        pltpu.make_async_copy(ref, ref, many.at[i]).wait()

    lax.fori_loop(0, 31, scatter, 0)
    sum_a.start_far()
    wait_many(1, tiles_in)
    tile = (tiles[q] + jnp.sum(tiles_in[...], axis=0)) * 0.25
    tile_out[...] = tile
    left_tiles[core, q] = tile
    lax.fori_loop(0, 31, gather, 0)
    sum_a.start_near()
    sum_a.middle()
    wait_many(3, tiles_in)
    swap = links.start(left_tiles.at[core], left_tiles.at[core], partner)
    swap.wait_recv()
    left = jnp.concatenate(
        [
            jnp.concatenate([left_tiles[h, 0:16].reshape(128, 128), left_tiles[h, 16:32].reshape(128, 128)], axis=1)
            for h in range(2)
        ],
        axis=0,
    )
    left_t[...] = left.T

    def ranks(p, h, part=None):
        n = SHARES[h]
        low, count = ((0, n), (0, n // 16 * 8 + 8), (n // 16 * 8 + 8, n - n // 16 * 8 - 8))[0 if part is None else part + 1]
        return pl.ds(pl.multiple_of((0, 4 * SHARES[0])[h] + n * p + low, 8), count)

    class Product:
        def __init__(self, cols, like, part, relay, landing, whole):
            self.cols, self.like, self.part, self.whole = cols, like, part, whole
            first = (0, SHARES[0])

            def rows(h):
                return slice(first[h], first[h] + SHARES[h])

            self.sum = RingSum(
                links, y, to_y, lambda p, h: part.at[ranks(p, h)],
                lambda h: relay.at[rows(h)], lambda i, h: landing.at[i, rows(h)], like.at[0, 0:192],
            )
            self.group_1, self.group_2 = links.group(like.at[0, 0:192]), links.group(like.at[0:3])
            self.from_place = {d: links.arrivals() for d in (1, 2, 3)}
            self.first = {d: links.arrivals() for d in range(4)}
            self.rest = links.arrivals()
            self.rings = {}

        def multiply(self):
            self.part[...] = dot3(left_t[...], summed[:, self.cols])

        def share(self):
            for h in range(2):
                piece = self.whole.at[x, ranks(y, h)]
                piece[...] = self.sum.finish(h)
                for d in (1, 3, 2):
                    there = to_y(lax.rem(y + d, 4)) if h == 0 else to_x(lax.rem(x + d, 4))
                    links.start(piece, piece, there, self.group_1, self.from_place[4 - d])
            self.pass_on(0)

        def pass_on(self, d):
            whole = self.whole
            from_y, from_x = lax.rem(y + d, 4), lax.rem(x + d, 4)
            sems = (self.group_2, self.first[d], self.rest)
            self.rings[d] = (
                RingGather(links, x, to_x, lambda p, i: whole.at[p, ranks(from_y, 0, i)], *sems),
                RingGather(links, y, to_y, lambda p, i: whole.at[from_x, ranks(p, 1, i)], *sems),
            )
            for ring in self.rings[d]:
                ring.start()

        def arrived(self, *places):
            for d in places:
                links.wait(self.from_place[d], self.like.at[0, 0:64])
                self.pass_on(d)

        def forward(self, *places):
            for d in places:
                links.wait(self.first[d], self.like.at[0, 0:64])
                for ring in self.rings[d]:
                    ring.forward()

        def finish(self):
            links.wait(self.rest, self.like.at[0:2])

    a = Product(slice(0, EARLY), early, part_a, relay_ta, landing_ta, all_a)
    b = Product(slice(EARLY, CHUNK), late, part_b, relay_tb, landing_tb, all_b)
    a.multiply()
    a.sum.start()
    slab = left_t[pl.ds(pl.multiple_of((core * 4 + x) * 32, 32), 32), :]
    gram_y[y] = dot(slab, left, precision=HIGHEST)
    grams = [links.start(gram_y.at[y], gram_y.at[y], to_y(lax.rem(y + d, 4))) for d in (2, 1, 3)]
    for h in range(2):
        summed[half(h), EARLY:CHUNK] = sum_a.finish(h)
    b.multiply()
    b.sum.start()
    a.sum.middle()
    for copy in grams:
        copy.wait_recv()
    gram_all[core, x] = (gram_y[0] + gram_y[1]) + (gram_y[2] + gram_y[3])
    grams = [links.start(gram_all.at[core, x], gram_all.at[core, x], to_x(lax.rem(x + d, 4))) for d in (2, 1, 3)]
    b.sum.middle()
    a.share()
    for copy in grams:
        copy.wait_recv()
    swap = links.start(gram_all.at[core], gram_all.at[core], partner)
    b.share()
    swap.wait_recv()
    for c in range(2):
        for p in range(4):
            chol[128 * c + 32 * p : 128 * c + 32 * p + 32, :] = gram_all[c, p]
    pieces = cholesky_pieces(chol, chol_x, chol_pivots)
    once = jnp.minimum(x + 1, 1)

    def work(n):
        now = [pieces.pop(0) for _ in range(n)]

        def step(i, carry):
            for piece in now:
                piece()
            return carry

        lax.fori_loop(0, once, step, 0)

    work(3)
    a.arrived(1, 3)
    work(3)
    b.arrived(1, 3)
    a.forward(0)
    a.arrived(2)
    work(3)
    b.arrived(2)
    b.forward(0)
    work(5)
    a.forward(1, 3)
    b.forward(1, 3)
    work(6)
    a.forward(2)
    b.forward(2)
    work(len(pieces))
    inverse = chol[...]
    ortho = dot(left, inverse, ((1,), (1,)), HIGHEST)
    ortho_out[...] = ortho

    ih, il = split(inverse * 0.25)
    sums = jnp.zeros((ROWS, 1), F32)
    for product, first, width in ((a, 0, EARLY), (b, EARLY_COLS, LATE)):
        product.finish()
        for p in range(4):
            th, tl = split(product.whole[p])
            right = dot(ih, th) + (dot(ih, tl) + dot(il, th))
            right_out[:, first + width * p : first + width * (p + 1)] = right
            sums = sums + jnp.sum(right * right, axis=1, keepdims=True)
    squares[f] = jnp.broadcast_to(sums, (ROWS, 128)).T[0:1]

    def share(i, carry):
        there = at(z=lax.rem(z + 4 + middle_out(i // 2), 8), core=lax.rem(core + 1 + i, 2))
        pltpu.make_async_remote_copy(
            src_ref=squares.at[f], dst_ref=squares.at[f], send_sem=many.at[4],
            recv_sem=many.at[5], device_id=there, device_id_type=MESH,
        ).start()
        return carry

    lax.fori_loop(0, 15, share, 0)
    basis = ortho.astype(BF16)
    rate = 1.0 - momentum_decay
    for p in range(4):
        cols = slice(EARLY * p, EARLY * (p + 1))
        momentum_out[:, cols] = early[p] - rate * dot(basis, right_out[:, cols].astype(BF16))
    cols = slice(EARLY_COLS, COLS)
    momentum_out[:, cols] = late_c[...] - rate * dot(basis, right_out[:, cols].astype(BF16))
    wait_many(5, squares.at[0:15])
    total = jnp.sum(squares[...], axis=0)
    scale_out[...] = jnp.broadcast_to(lax.rsqrt(total / TOTAL_COLS + norm_eps), (8, ROWS))
    wait_many(0, tiles_in)
    wait_many(2, tiles_in)
    wait_many(4, squares.at[0:15])
    links.drain()
    assert links.sends <= SENDS and links.recvs <= ARRIVALS


def exchange(momentum, gradient, right_t):
    vmem = lambda *shape: pltpu.VMEM(shape, F32)
    return pl.pallas_call(
        exchange_kernel,
        out_shape=(
            jax.ShapeDtypeStruct((ROWS, COLS), F32),
            jax.ShapeDtypeStruct((ROWS, ROWS), F32),
            jax.ShapeDtypeStruct((8, ROWS), F32),
            jax.ShapeDtypeStruct((ROWS, COLS), F32),
        ),
        in_specs=[pl.BlockSpec(memory_space=pltpu.HBM)] * 3,
        out_specs=(pl.BlockSpec(memory_space=pltpu.VMEM),) * 4,
        scratch_shapes=[
            vmem(4, ROWS, EARLY),
            vmem(4, ROWS, EARLY),
            vmem(ROWS, LATE_COLS),
            vmem(ROWS, LATE_COLS),
            vmem(4, ROWS, LATE),
            vmem(64, COLS),
            vmem(ROWS, EARLY),
            vmem(ROWS, LATE_COLS),
            vmem(ROWS, CHUNK),
            vmem(2, 128, EARLY),
            vmem(2, 2, 128, EARLY),
            vmem(2, 128, LATE),
            vmem(2, 2, 128, LATE),
            vmem(2, 128, ROWS),
            vmem(128, ROWS),
            vmem(32, 8, 128),
            vmem(31, 8, 128),
            vmem(8, 128),
            vmem(2, 32, 8, 128),
            vmem(ROWS, ROWS),
            vmem(4, 32, ROWS),
            vmem(2, 4, 32, ROWS),
            vmem(ROWS, ROWS),
            vmem(NB, 128),
            vmem(NB, 128),
            vmem(ROWS, EARLY),
            vmem(64, EARLY),
            vmem(2, 64, EARLY),
            vmem(4, ROWS, EARLY),
            vmem(ROWS, LATE),
            vmem(64, LATE),
            vmem(2, 64, LATE),
            vmem(4, ROWS, LATE),
            vmem(16, 1, ROWS),
            pltpu.SemaphoreType.DMA((SENDS,)),
            pltpu.SemaphoreType.DMA((ARRIVALS,)),
            pltpu.SemaphoreType.DMA((11,)),
            pltpu.SemaphoreType.DMA((6,)),
        ],
        compiler_params=pltpu.CompilerParams(
            collective_id=0, has_side_effects=True, vmem_limit_bytes=45 * 1024 * 1024
        ),
        cost_estimate=pl.CostEstimate(flops=4 * 2 * ROWS * ROWS * COLS, bytes_accessed=11_000_000, transcendentals=0),
        name="exchange",
    )(momentum, gradient, right_t)


def update_kernel(
    ortho, scale, right, weights, momentum, new_weights, new_momentum, new_right, staged_w, column_ref, staged_r, sems
):
    copies = [pltpu.make_async_copy(momentum, new_momentum, sems.at[0])]
    copies[0].start()
    own = pl.ds(pl.multiple_of(lax.axis_index("tp") * 64, 64), 64)
    sh, sl = split(ortho[...] * scale[0:1, :])
    column_ref[...] = jnp.broadcast_to(scale[0:1, :], (128, ROWS)).T
    column = column_ref[own, :]
    column = jnp.concatenate([column] * (WIDTH // 128), axis=1)
    for i in range(COLS // WIDTH):
        cols = slice(WIDTH * i, WIDTH * (i + 1))
        rh, rl = split(right[:, cols])
        normal = dot(sh, rh) + (dot(sh, rl) + dot(sl, rh))
        staged_w[:, cols] = weights[:, cols] - learning_rate * normal
        staged_r[:, cols] = column * right[own, cols]
        copies.append(pltpu.make_async_copy(staged_w.at[:, cols], new_weights.at[:, cols], sems.at[2 * i + 1]))
        copies[-1].start()
        copies.append(
            pltpu.make_async_copy(staged_r.at[:, cols], new_right.at[:, cols], sems.at[2 * i + 2])
        )
        copies[-1].start()
    for copy in copies:
        copy.wait()


WIDTH = 1664


def update(ortho, scale, right, weights, momentum):
    return pl.pallas_call(
        update_kernel,
        out_shape=(
            jax.ShapeDtypeStruct((ROWS, COLS), F32),
            jax.ShapeDtypeStruct((ROWS, COLS), F32),
            jax.ShapeDtypeStruct((64, COLS), F32),
        ),
        in_specs=[pl.BlockSpec(memory_space=pltpu.VMEM)] * 5,
        out_specs=(pl.BlockSpec(memory_space=pltpu.HBM),) * 3,
        scratch_shapes=[
            pltpu.VMEM((ROWS, COLS), F32),
            pltpu.VMEM((ROWS, 128), F32),
            pltpu.VMEM((64, COLS), F32),
            pltpu.SemaphoreType.DMA((2 * (COLS // WIDTH) + 1,)),
        ],
        compiler_params=pltpu.CompilerParams(vmem_limit_bytes=40 * 1024 * 1024),
        name="update",
    )(ortho, scale, right, weights, momentum)


def local(weights, momentum, gradient, right_factor):
    right, ortho, scale, moved = exchange(momentum, gradient, right_factor.T)
    new_weights, new_momentum, new_right_t = update(ortho, scale, right, weights, moved)
    return (new_weights, new_momentum, new_right_t.T)


def solution(mesh):
    return jax.shard_map(
        local,
        mesh=mesh,
        in_specs=(
            P("tp", "fsdp"),
            P(("rep", "tp"), "fsdp"),
            P(("rep", "tp"), "fsdp"),
            P("fsdp", "tp"),
        ),
        out_specs=(P("tp", "fsdp"), P(("rep", "tp"), "fsdp"), P("fsdp", "tp")),
        check_vma=False,
    )
```

```python
import functools

import jax
import jax.numpy as jnp
from jax import lax
from jax.experimental import pallas as pl
from jax.experimental.pallas import tpu as pltpu
from jax.sharding import PartitionSpec as P

MESH = pl.DeviceIdType.MESH
HIGHEST = lax.Precision.HIGHEST
F32 = jnp.float32
BF16 = jnp.bfloat16

momentum_decay = 0.95
learning_rate = 0.05
norm_eps = 1e-06

ROWS = 256
COLS = 3328
CHUNK = 832
EARLY = 512
LATE = CHUNK - EARLY
EARLY_COLS = 4 * EARLY
LATE_COLS = 4 * LATE
TOTAL_COLS = 53248
SHARES = (32, 32)
SENDS, ARRIVALS = 19, 53
NB = 64
STEP = 8


def dot(a, b, dims=((1,), (0,)), precision=None):
    return lax.dot_general(a, b, (dims, ((), ())), precision=precision, preferred_element_type=F32)


def split(a):
    high = a.astype(BF16)
    return high, (a - high.astype(F32)).astype(BF16)


def dot3(a, b, dims=((1,), (0,))):
    ah, al = split(a)
    bh, bl = split(b)
    return dot(ah, bh, dims) + (dot(ah, bl, dims) + dot(al, bh, dims))


def cholesky_pieces(m_ref, x_ref, pivots_ref):
    n = ROWS
    rows = lax.broadcasted_iota(jnp.int32, (NB, 128), 0)
    cols = lax.broadcasted_iota(jnp.int32, (NB, 128), 1)
    eye = jnp.where(cols == rows + 64, 1.0, 0.0).astype(F32)

    def pivots_from(j):
        if j == 0:
            x_ref[...] = jnp.concatenate([m_ref[0:NB, 0:NB], jnp.zeros((NB, 128 - NB), F32)], axis=1) + eye
        x = x_ref[...]
        pivots = pivots_ref[...]
        c = [jnp.broadcast_to(x[:, j + b : j + b + 1], (NB, 128)) for b in range(STEP)]
        r = [x[j + a : j + a + 1, :] for a in range(STEP)]
        update = None
        for b in range(STEP):
            pivot = c[b][j + b : j + b + 1, :]
            pivots = jnp.where(rows == j + b, pivot, pivots)
            factor = jnp.where(rows > j + b, c[b] * (1.0 / pivot), 0.0)
            for later in range(b + 1, STEP):
                c[later] = c[later] - factor * c[later][j + b : j + b + 1, :]
                r[later] = r[later] - factor[j + later : j + later + 1, :] * r[b]
            term = factor * r[b]
            update = term if update is None else update + term
        x_ref[...] = x - update
        pivots_ref[...] = pivots

    def rest(block):
        w = (x_ref[...] * lax.rsqrt(pivots_ref[...]))[:, 64 : 64 + NB]
        m = m_ref[...]
        col = lax.broadcasted_iota(jnp.int32, (n, n), 1)
        top = dot(w, m[0:NB, :], precision=HIGHEST)
        top = jnp.concatenate([w, top[:, NB:]], axis=1)
        below = dot(m[:, 0:NB], w, ((1,), (1,)), HIGHEST)
        row = lax.broadcasted_iota(jnp.int32, (n, NB), 0)
        below = jnp.where((row >= NB) & (row < n - NB * block), below, 0.0)
        new = jnp.where(col < NB, 0.0, m) - dot(below, top, precision=HIGHEST)
        new = jnp.concatenate([new[NB:], top], axis=0)
        m_ref[...] = jnp.concatenate([new[:, NB:], new[:, :NB]], axis=1)

    pieces = []
    for block in range(n // NB):
        pieces += [functools.partial(pivots_from, j) for j in range(0, NB, STEP)]
        pieces.append(functools.partial(rest, block))
    return pieces


class Links:
    def __init__(self, send, recv):
        self.send, self.recv, self.sends, self.recvs, self.at_end = send, recv, 0, 0, []

    def wait(self, sem, ref):
        pltpu.make_async_copy(ref, ref, sem).wait()

    def group(self, ref):
        sem = self.send.at[self.sends]
        self.sends += 1
        self.at_end.append(lambda: self.wait(sem, ref))
        return sem

    def arrivals(self):
        sem = self.recv.at[self.recvs]
        self.recvs += 1
        return sem

    def start(self, src, dst, device, group=None, arrivals=None):
        alone = group is None
        if alone:
            group = self.send.at[self.sends]
            self.sends += 1
        copy = pltpu.make_async_remote_copy(
            src_ref=src,
            dst_ref=dst,
            send_sem=group,
            recv_sem=self.arrivals() if arrivals is None else arrivals,
            device_id=device,
            device_id_type=MESH,
        )
        copy.start()
        if alone:
            self.at_end.append(copy.wait_send)
        return copy

    def drain(self):
        for wait in self.at_end:
            wait()


class RingSum:
    def __init__(self, links, me, to, part, relay, landing, sent):
        self.links, self.me, self.to, self.part = links, me, to, part
        self.relay, self.landing = relay, landing
        self.right, self.left, self.far = (lax.rem(me + d, 4) for d in (1, 3, 2))
        self.group = links.group(sent)

    def go(self, src, dst, place):
        return self.links.start(src, dst, self.to(place), self.group)

    def start(self):
        self.start_far()
        self.start_near()

    def start_far(self):
        self.a = self.go(self.part(self.far, 0), self.relay(0), self.right)
        self.b = self.go(self.part(self.far, 1), self.relay(1), self.left)

    def start_near(self):
        self.c = self.go(self.part(self.right, 1), self.landing(0, 1), self.right)
        self.d = self.go(self.part(self.left, 0), self.landing(1, 0), self.left)

    def middle(self):
        self.a.wait_recv()
        ref = self.relay(0)
        ref[...] = ref[...] + self.part(self.right, 0)[...]
        self.e = self.go(ref, self.landing(0, 0), self.right)
        self.b.wait_recv()
        ref = self.relay(1)
        ref[...] = ref[...] + self.part(self.left, 1)[...]
        self.f = self.go(ref, self.landing(1, 1), self.left)

    def finish(self, half):
        for copy in (self.d, self.e) if half == 0 else (self.c, self.f):
            copy.wait_recv()
        return self.part(self.me, half)[...] + (self.landing(0, half)[...] + self.landing(1, half)[...])


class RingGather:
    def __init__(self, links, me, to, part, group, first, rest):
        self.links, self.me, self.to, self.part = links, me, to, part
        self.group, self.first, self.rest = group, first, rest
        self.right, self.left = lax.rem(me + 1, 4), lax.rem(me + 3, 4)

    def go(self, place, half, device, arrivals):
        ref = self.part(place, half)
        self.links.start(ref, ref, self.to(device), self.group, arrivals)

    def start(self):
        self.go(self.me, 0, self.right, self.first)
        self.go(self.me, 1, self.left, self.first)
        self.go(self.me, 1, self.right, self.rest)
        self.go(self.me, 0, self.left, self.rest)

    def forward(self):
        self.go(self.left, 0, self.right, self.rest)
        self.go(self.right, 1, self.left, self.rest)


def exchange_kernel(
    momentum, gradient, right_in, right_out, ortho_out, scale_out, momentum_out,
    early, early_g, late_c, late_g, late, rown, rearly, rlate, summed, relay_b, landing_b, relay_a, landing_a,
    part_left, core_in, tiles, tiles_in, tile_out, left_tiles, left_t,
    gram_y, gram_all, chol, chol_x, chol_pivots, part_a, relay_ta, landing_ta, all_a,
    part_b, relay_tb, landing_tb, all_b, squares,
    send, recv, load, many,
):
    x, f, y = lax.axis_index("rep"), lax.axis_index("fsdp"), lax.axis_index("tp")
    z, core = f // 2, lax.rem(f, 2)
    q = x * 8 + z

    def at(x=x, z=z, core=core, y=y):
        return {"rep": x, "fsdp": z * 2 + core, "tp": y}

    def middle_out(i):
        return ((i + 1) // 2) * (1 - 2 * lax.rem(i, 2))

    def plane(i):
        there_x = lax.rem(x + 2 + middle_out(lax.rem(i, 4)), 4)
        there_z = lax.rem(z + 4 + middle_out(i // 4), 8)
        return there_x * 8 + there_z, at(x=there_x, z=there_z)

    to_x = lambda p: at(x=p)
    to_y = lambda p: at(y=p)
    partner = at(core=1 - core)
    links = Links(send, recv)

    load_r = pltpu.make_async_copy(right_in, rown, load.at[0])
    load_r.start()
    order = [lax.rem(x + d, 4) for d in (2, 1, 3, 0)]
    loads = []
    for i, p in enumerate(order):
        cols = pl.ds(pl.multiple_of(EARLY * p, EARLY), EARLY)
        loads.append(
            (
                pltpu.make_async_copy(momentum.at[:, cols], early.at[p], load.at[1 + 2 * i]),
                pltpu.make_async_copy(gradient.at[:, cols], early_g.at[p], load.at[2 + 2 * i]),
            )
        )
    loads.append(
        (
            pltpu.make_async_copy(momentum.at[:, EARLY_COLS:COLS], late_c, load.at[9]),
            pltpu.make_async_copy(gradient.at[:, EARLY_COLS:COLS], late_g, load.at[10]),
        )
    )
    for pair in loads[:4]:
        for copy in pair:
            copy.start()

    def loaded(i):
        for copy in loads[i]:
            copy.wait()
        early[order[i]] = early[order[i]] + early_g[order[i]]

    barrier = pltpu.get_barrier_semaphore()

    def greet(d, carry):
        pl.semaphore_signal(barrier, inc=1, device_id=plane(d)[1], device_id_type=MESH)
        return carry

    for d in (1, 2, 3):
        pl.semaphore_signal(barrier, inc=1, device_id=to_y(lax.rem(y + d, 4)), device_id_type=MESH)
    pl.semaphore_signal(barrier, inc=1, device_id=partner, device_id_type=MESH)
    lax.fori_loop(0, 31, greet, 0)

    my_ranks = pl.ds(pl.multiple_of(64 * y, 64), 64)
    load_r.wait()
    rearly[my_ranks, :] = rown[:, pl.ds(pl.multiple_of(EARLY * x, EARLY), EARLY)]
    rlate[my_ranks, :] = rown[:, EARLY_COLS:COLS]
    loaded(0)
    pl.semaphore_wait(barrier, 35)

    def rank_rows(p, h):
        return pl.ds(pl.multiple_of(64 * p + 32 * h, 32), 32)

    def half(h):
        return slice(128 * h, 128 * (h + 1))

    sum_b = RingSum(
        links, x, to_x, lambda p, h: early.at[p, half(h)],
        lambda h: relay_b.at[h], lambda i, h: landing_b.at[i, h], early.at[0:3],
    )
    gathers = []
    for ref in (rlate, rearly):
        sems = (links.group(ref.at[0:192]), links.arrivals(), links.arrivals())
        gathers.append(RingGather(links, y, to_y, lambda p, h, ref=ref: ref.at[rank_rows(p, h)], *sems))
    gather_a, gather_b = gathers
    sum_b.start_far()
    gather_a.start()
    gather_b.start()
    loaded(1)
    loaded(2)
    sum_b.start_near()
    for copy in loads[4]:
        copy.start()
    loaded(3)
    for copy in loads[4]:
        copy.wait()
    late_c[...] = late_c[...] + late_g[...]
    for p in range(4):
        late[p] = late_c[:, LATE * p : LATE * (p + 1)]
    links.wait(gather_a.first, rlate.at[0:64])
    gather_a.forward()
    sum_b.middle()
    links.wait(gather_b.first, rearly.at[0:64])
    gather_b.forward()
    links.wait(gather_a.rest, rlate.at[0:128])
    total = dot3(late_c[...], rlate[...], ((1,), (1,)))
    links.wait(gather_b.rest, rearly.at[0:128])
    for h in range(2):
        summed[half(h), 0:EARLY] = sum_b.finish(h)
    total = total + dot3(summed[:, 0:EARLY], rearly[...], ((1,), (1,)))
    part_left[0] = total[0:128]
    part_left[1] = total[128:256]

    swap = links.start(part_left.at[1 - core], core_in, partner)
    sum_a = RingSum(
        links, x, to_x, lambda p, h: late.at[p, half(h)],
        lambda h: relay_a.at[h], lambda i, h: landing_a.at[i, h], late.at[0:3],
    )
    swap.wait_recv()
    mine = part_left[core] + core_in[...]
    tiles[0:16] = mine[:, 0:128].reshape(16, 8, 128)
    tiles[16:32] = mine[:, 128:256].reshape(16, 8, 128)

    def scatter(d, carry):
        other, device = plane(d)
        pltpu.make_async_remote_copy(
            src_ref=tiles.at[other], dst_ref=tiles_in.at[d], send_sem=many.at[0],
            recv_sem=many.at[1], device_id=device, device_id_type=MESH,
        ).start()
        return carry

    def gather(d, carry):
        pltpu.make_async_remote_copy(
            src_ref=tile_out, dst_ref=left_tiles.at[core, q], send_sem=many.at[2],
            recv_sem=many.at[3], device_id=plane(d)[1], device_id_type=MESH,
        ).start()
        return carry

    def wait_many(i, ref):
        pltpu.make_async_copy(ref, ref, many.at[i]).wait()

    lax.fori_loop(0, 31, scatter, 0)
    sum_a.start_far()
    wait_many(1, tiles_in)
    tile = (tiles[q] + jnp.sum(tiles_in[...], axis=0)) * 0.25
    tile_out[...] = tile
    left_tiles[core, q] = tile
    lax.fori_loop(0, 31, gather, 0)
    sum_a.start_near()
    sum_a.middle()
    wait_many(3, tiles_in)
    swap = links.start(left_tiles.at[core], left_tiles.at[core], partner)
    swap.wait_recv()
    left = jnp.concatenate(
        [
            jnp.concatenate([left_tiles[h, 0:16].reshape(128, 128), left_tiles[h, 16:32].reshape(128, 128)], axis=1)
            for h in range(2)
        ],
        axis=0,
    )
    left_t[...] = left.T

    def ranks(p, h, part=None):
        n = SHARES[h]
        low, count = ((0, n), (0, n // 16 * 8 + 8), (n // 16 * 8 + 8, n - n // 16 * 8 - 8))[0 if part is None else part + 1]
        return pl.ds(pl.multiple_of((0, 4 * SHARES[0])[h] + n * p + low, 8), count)

    class Product:
        def __init__(self, cols, like, part, relay, landing, whole):
            self.cols, self.like, self.part, self.whole = cols, like, part, whole
            first = (0, SHARES[0])

            def rows(h):
                return slice(first[h], first[h] + SHARES[h])

            self.sum = RingSum(
                links, y, to_y, lambda p, h: part.at[ranks(p, h)],
                lambda h: relay.at[rows(h)], lambda i, h: landing.at[i, rows(h)], like.at[0, 0:192],
            )
            self.group_1, self.group_2 = links.group(like.at[0, 0:192]), links.group(like.at[0:3])
            self.from_place = {d: links.arrivals() for d in (1, 2, 3)}
            self.first = {d: links.arrivals() for d in range(4)}
            self.rest = links.arrivals()
            self.rings = {}

        def multiply(self):
            self.part[...] = dot3(left_t[...], summed[:, self.cols])

        def share(self):
            for h in range(2):
                piece = self.whole.at[x, ranks(y, h)]
                piece[...] = self.sum.finish(h)
                for d in (1, 3, 2):
                    there = to_y(lax.rem(y + d, 4)) if h == 0 else to_x(lax.rem(x + d, 4))
                    links.start(piece, piece, there, self.group_1, self.from_place[4 - d])
            self.pass_on(0)

        def pass_on(self, d):
            whole = self.whole
            from_y, from_x = lax.rem(y + d, 4), lax.rem(x + d, 4)
            sems = (self.group_2, self.first[d], self.rest)
            self.rings[d] = (
                RingGather(links, x, to_x, lambda p, i: whole.at[p, ranks(from_y, 0, i)], *sems),
                RingGather(links, y, to_y, lambda p, i: whole.at[from_x, ranks(p, 1, i)], *sems),
            )
            for ring in self.rings[d]:
                ring.start()

        def arrived(self, *places):
            for d in places:
                links.wait(self.from_place[d], self.like.at[0, 0:64])
                self.pass_on(d)

        def forward(self, *places):
            for d in places:
                links.wait(self.first[d], self.like.at[0, 0:64])
                for ring in self.rings[d]:
                    ring.forward()

        def finish(self):
            links.wait(self.rest, self.like.at[0:2])

    a = Product(slice(0, EARLY), early, part_a, relay_ta, landing_ta, all_a)
    b = Product(slice(EARLY, CHUNK), late, part_b, relay_tb, landing_tb, all_b)
    a.multiply()
    a.sum.start()
    slab = left_t[pl.ds(pl.multiple_of((core * 4 + x) * 32, 32), 32), :]
    gram_y[y] = dot(slab, left, precision=HIGHEST)
    grams = [links.start(gram_y.at[y], gram_y.at[y], to_y(lax.rem(y + d, 4))) for d in (2, 1, 3)]
    for h in range(2):
        summed[half(h), EARLY:CHUNK] = sum_a.finish(h)
    b.multiply()
    b.sum.start()
    a.sum.middle()
    for copy in grams:
        copy.wait_recv()
    gram_all[core, x] = (gram_y[0] + gram_y[1]) + (gram_y[2] + gram_y[3])
    grams = [links.start(gram_all.at[core, x], gram_all.at[core, x], to_x(lax.rem(x + d, 4))) for d in (2, 1, 3)]
    b.sum.middle()
    a.share()
    for copy in grams:
        copy.wait_recv()
    swap = links.start(gram_all.at[core], gram_all.at[core], partner)
    b.share()
    swap.wait_recv()
    for c in range(2):
        for p in range(4):
            chol[128 * c + 32 * p : 128 * c + 32 * p + 32, :] = gram_all[c, p]
    pieces = cholesky_pieces(chol, chol_x, chol_pivots)
    once = jnp.minimum(x + 1, 1)

    def work(n):
        now = [pieces.pop(0) for _ in range(n)]

        def step(i, carry):
            for piece in now:
                piece()
            return carry

        lax.fori_loop(0, once, step, 0)

    work(3)
    a.arrived(1, 3)
    work(3)
    b.arrived(1, 3)
    a.forward(0)
    a.arrived(2)
    work(3)
    b.arrived(2)
    b.forward(0)
    work(5)
    a.forward(1, 3)
    b.forward(1, 3)
    work(6)
    a.forward(2)
    b.forward(2)
    work(len(pieces))
    inverse = chol[...]
    ortho = dot(left, inverse, ((1,), (1,)), HIGHEST)
    ortho_out[...] = ortho

    ih, il = split(inverse * 0.25)
    sums = jnp.zeros((ROWS, 1), F32)
    for product, first, width in ((a, 0, EARLY), (b, EARLY_COLS, LATE)):
        product.finish()
        for p in range(4):
            th, tl = split(product.whole[p])
            right = dot(ih, th) + (dot(ih, tl) + dot(il, th))
            right_out[:, first + width * p : first + width * (p + 1)] = right
            sums = sums + jnp.sum(right * right, axis=1, keepdims=True)
    squares[f] = jnp.broadcast_to(sums, (ROWS, 128)).T[0:1]

    def share(i, carry):
        there = at(z=lax.rem(z + 4 + middle_out(i // 2), 8), core=lax.rem(core + 1 + i, 2))
        pltpu.make_async_remote_copy(
            src_ref=squares.at[f], dst_ref=squares.at[f], send_sem=many.at[4],
            recv_sem=many.at[5], device_id=there, device_id_type=MESH,
        ).start()
        return carry

    lax.fori_loop(0, 15, share, 0)
    basis = ortho.astype(BF16)
    rate = 1.0 - momentum_decay
    for p in range(4):
        cols = slice(EARLY * p, EARLY * (p + 1))
        momentum_out[:, cols] = early[p] - rate * dot(basis, right_out[:, cols].astype(BF16))
    cols = slice(EARLY_COLS, COLS)
    momentum_out[:, cols] = late_c[...] - rate * dot(basis, right_out[:, cols].astype(BF16))
    wait_many(5, squares.at[0:15])
    total = jnp.sum(squares[...], axis=0)
    scale_out[...] = jnp.broadcast_to(lax.rsqrt(total / TOTAL_COLS + norm_eps), (8, ROWS))
    wait_many(0, tiles_in)
    wait_many(2, tiles_in)
    wait_many(4, squares.at[0:15])
    links.drain()
    assert links.sends <= SENDS and links.recvs <= ARRIVALS


def exchange(momentum, gradient, right_t):
    vmem = lambda *shape: pltpu.VMEM(shape, F32)
    return pl.pallas_call(
        exchange_kernel,
        out_shape=(
            jax.ShapeDtypeStruct((ROWS, COLS), F32),
            jax.ShapeDtypeStruct((ROWS, ROWS), F32),
            jax.ShapeDtypeStruct((8, ROWS), F32),
            jax.ShapeDtypeStruct((ROWS, COLS), F32),
        ),
        in_specs=[pl.BlockSpec(memory_space=pltpu.HBM)] * 3,
        out_specs=(pl.BlockSpec(memory_space=pltpu.VMEM),) * 4,
        scratch_shapes=[
            vmem(4, ROWS, EARLY),
            vmem(4, ROWS, EARLY),
            vmem(ROWS, LATE_COLS),
            vmem(ROWS, LATE_COLS),
            vmem(4, ROWS, LATE),
            vmem(64, COLS),
            vmem(ROWS, EARLY),
            vmem(ROWS, LATE_COLS),
            vmem(ROWS, CHUNK),
            vmem(2, 128, EARLY),
            vmem(2, 2, 128, EARLY),
            vmem(2, 128, LATE),
            vmem(2, 2, 128, LATE),
            vmem(2, 128, ROWS),
            vmem(128, ROWS),
            vmem(32, 8, 128),
            vmem(31, 8, 128),
            vmem(8, 128),
            vmem(2, 32, 8, 128),
            vmem(ROWS, ROWS),
            vmem(4, 32, ROWS),
            vmem(2, 4, 32, ROWS),
            vmem(ROWS, ROWS),
            vmem(NB, 128),
            vmem(NB, 128),
            vmem(ROWS, EARLY),
            vmem(64, EARLY),
            vmem(2, 64, EARLY),
            vmem(4, ROWS, EARLY),
            vmem(ROWS, LATE),
            vmem(64, LATE),
            vmem(2, 64, LATE),
            vmem(4, ROWS, LATE),
            vmem(16, 1, ROWS),
            pltpu.SemaphoreType.DMA((SENDS,)),
            pltpu.SemaphoreType.DMA((ARRIVALS,)),
            pltpu.SemaphoreType.DMA((11,)),
            pltpu.SemaphoreType.DMA((6,)),
        ],
        compiler_params=pltpu.CompilerParams(
            collective_id=0, has_side_effects=True, vmem_limit_bytes=45 * 1024 * 1024
        ),
        cost_estimate=pl.CostEstimate(flops=4 * 2 * ROWS * ROWS * COLS, bytes_accessed=11_000_000, transcendentals=0),
        name="exchange",
    )(momentum, gradient, right_t)


def update_kernel(
    ortho, scale, right, weights, momentum, new_weights, new_momentum, new_right, staged_w, column_ref, staged_r, sems
):
    copies = [pltpu.make_async_copy(momentum, new_momentum, sems.at[0])]
    copies[0].start()
    own = pl.ds(pl.multiple_of(lax.axis_index("tp") * 64, 64), 64)
    sh, sl = split(ortho[...] * scale[0:1, :])
    column_ref[...] = jnp.broadcast_to(scale[0:1, :], (128, ROWS)).T
    column = column_ref[own, :]
    column = jnp.concatenate([column] * (WIDTH // 128), axis=1)
    for i in range(COLS // WIDTH):
        cols = slice(WIDTH * i, WIDTH * (i + 1))
        rh, rl = split(right[:, cols])
        normal = dot(sh, rh) + (dot(sh, rl) + dot(sl, rh))
        staged_w[:, cols] = weights[:, cols] - learning_rate * normal
        staged_r[:, cols] = column * right[own, cols]
        copies.append(pltpu.make_async_copy(staged_w.at[:, cols], new_weights.at[:, cols], sems.at[2 * i + 1]))
        copies[-1].start()
        copies.append(
            pltpu.make_async_copy(staged_r.at[:, cols], new_right.at[:, cols], sems.at[2 * i + 2])
        )
        copies[-1].start()
    for copy in copies:
        copy.wait()


WIDTH = 1664


def update(ortho, scale, right, weights, momentum):
    return pl.pallas_call(
        update_kernel,
        out_shape=(
            jax.ShapeDtypeStruct((ROWS, COLS), F32),
            jax.ShapeDtypeStruct((ROWS, COLS), F32),
            jax.ShapeDtypeStruct((64, COLS), F32),
        ),
        in_specs=[pl.BlockSpec(memory_space=pltpu.VMEM)] * 5,
        out_specs=(pl.BlockSpec(memory_space=pltpu.HBM),) * 3,
        scratch_shapes=[
            pltpu.VMEM((ROWS, COLS), F32),
            pltpu.VMEM((ROWS, 128), F32),
            pltpu.VMEM((64, COLS), F32),
            pltpu.SemaphoreType.DMA((2 * (COLS // WIDTH) + 1,)),
        ],
        compiler_params=pltpu.CompilerParams(vmem_limit_bytes=40 * 1024 * 1024),
        name="update",
    )(ortho, scale, right, weights, momentum)


def local(weights, momentum, gradient, right_factor):
    right, ortho, scale, moved = exchange(momentum, gradient, right_factor.T)
    new_weights, new_momentum, new_right_t = update(ortho, scale, right, weights, moved)
    return (new_weights, new_momentum, new_right_t.T)


def solution(mesh):
    return jax.shard_map(
        local,
        mesh=mesh,
        in_specs=(
            P("tp", "fsdp"),
            P(("rep", "tp"), "fsdp"),
            P(("rep", "tp"), "fsdp"),
            P("fsdp", "tp"),
        ),
        out_specs=(P("tp", "fsdp"), P(("rep", "tp"), "fsdp"), P("fsdp", "tp")),
        check_vma=False,
    )
```

```python
import functools

import jax
import jax.numpy as jnp
from jax import lax
from jax.experimental import pallas as pl
from jax.experimental.pallas import tpu as pltpu
from jax.sharding import PartitionSpec as P

MESH = pl.DeviceIdType.MESH
HIGHEST = lax.Precision.HIGHEST
F32 = jnp.float32
BF16 = jnp.bfloat16

momentum_decay = 0.95
learning_rate = 0.05
norm_eps = 1e-06

ROWS = 256
COLS = 3328
CHUNK = 832
EARLY = 512
LATE = CHUNK - EARLY
EARLY_COLS = 4 * EARLY
LATE_COLS = 4 * LATE
TOTAL_COLS = 53248
SHARES = (32, 32)
SENDS, ARRIVALS = 19, 53
NB = 64
STEP = 8


def dot(a, b, dims=((1,), (0,)), precision=None):
    return lax.dot_general(a, b, (dims, ((), ())), precision=precision, preferred_element_type=F32)


def split(a):
    high = a.astype(BF16)
    return high, (a - high.astype(F32)).astype(BF16)


def dot3(a, b, dims=((1,), (0,))):
    ah, al = split(a)
    bh, bl = split(b)
    return dot(ah, bh, dims) + (dot(ah, bl, dims) + dot(al, bh, dims))


def cholesky_pieces(m_ref, x_ref, pivots_ref):
    n = ROWS
    rows = lax.broadcasted_iota(jnp.int32, (NB, 128), 0)
    cols = lax.broadcasted_iota(jnp.int32, (NB, 128), 1)
    eye = jnp.where(cols == rows + 64, 1.0, 0.0).astype(F32)

    def pivots_from(j):
        if j == 0:
            x_ref[...] = jnp.concatenate([m_ref[0:NB, 0:NB], jnp.zeros((NB, 128 - NB), F32)], axis=1) + eye
        x = x_ref[...]
        pivots = pivots_ref[...]
        c = [jnp.broadcast_to(x[:, j + b : j + b + 1], (NB, 128)) for b in range(STEP)]
        r = [x[j + a : j + a + 1, :] for a in range(STEP)]
        update = None
        for b in range(STEP):
            pivot = c[b][j + b : j + b + 1, :]
            pivots = jnp.where(rows == j + b, pivot, pivots)
            factor = jnp.where(rows > j + b, c[b] * (1.0 / pivot), 0.0)
            for later in range(b + 1, STEP):
                c[later] = c[later] - factor * c[later][j + b : j + b + 1, :]
                r[later] = r[later] - factor[j + later : j + later + 1, :] * r[b]
            term = factor * r[b]
            update = term if update is None else update + term
        x_ref[...] = x - update
        pivots_ref[...] = pivots

    def rest(block):
        w = (x_ref[...] * lax.rsqrt(pivots_ref[...]))[:, 64 : 64 + NB]
        m = m_ref[...]
        col = lax.broadcasted_iota(jnp.int32, (n, n), 1)
        top = dot(w, m[0:NB, :], precision=HIGHEST)
        top = jnp.concatenate([w, top[:, NB:]], axis=1)
        below = dot(m[:, 0:NB], w, ((1,), (1,)), HIGHEST)
        row = lax.broadcasted_iota(jnp.int32, (n, NB), 0)
        below = jnp.where((row >= NB) & (row < n - NB * block), below, 0.0)
        new = jnp.where(col < NB, 0.0, m) - dot(below, top, precision=HIGHEST)
        new = jnp.concatenate([new[NB:], top], axis=0)
        m_ref[...] = jnp.concatenate([new[:, NB:], new[:, :NB]], axis=1)

    pieces = []
    for block in range(n // NB):
        pieces += [functools.partial(pivots_from, j) for j in range(0, NB, STEP)]
        pieces.append(functools.partial(rest, block))
    return pieces


class Links:
    def __init__(self, send, recv):
        self.send, self.recv, self.sends, self.recvs, self.at_end = send, recv, 0, 0, []

    def wait(self, sem, ref):
        pltpu.make_async_copy(ref, ref, sem).wait()

    def group(self, ref):
        sem = self.send.at[self.sends]
        self.sends += 1
        self.at_end.append(lambda: self.wait(sem, ref))
        return sem

    def arrivals(self):
        sem = self.recv.at[self.recvs]
        self.recvs += 1
        return sem

    def start(self, src, dst, device, group=None, arrivals=None):
        alone = group is None
        if alone:
            group = self.send.at[self.sends]
            self.sends += 1
        copy = pltpu.make_async_remote_copy(
            src_ref=src,
            dst_ref=dst,
            send_sem=group,
            recv_sem=self.arrivals() if arrivals is None else arrivals,
            device_id=device,
            device_id_type=MESH,
        )
        copy.start()
        if alone:
            self.at_end.append(copy.wait_send)
        return copy

    def drain(self):
        for wait in self.at_end:
            wait()


class RingSum:
    def __init__(self, links, me, to, part, relay, landing, sent):
        self.links, self.me, self.to, self.part = links, me, to, part
        self.relay, self.landing = relay, landing
        self.right, self.left, self.far = (lax.rem(me + d, 4) for d in (1, 3, 2))
        self.group = links.group(sent)

    def go(self, src, dst, place):
        return self.links.start(src, dst, self.to(place), self.group)

    def start(self):
        self.start_far()
        self.start_near()

    def start_far(self):
        self.a = self.go(self.part(self.far, 0), self.relay(0), self.right)
        self.b = self.go(self.part(self.far, 1), self.relay(1), self.left)

    def start_near(self):
        self.c = self.go(self.part(self.right, 1), self.landing(0, 1), self.right)
        self.d = self.go(self.part(self.left, 0), self.landing(1, 0), self.left)

    def middle(self):
        self.a.wait_recv()
        ref = self.relay(0)
        ref[...] = ref[...] + self.part(self.right, 0)[...]
        self.e = self.go(ref, self.landing(0, 0), self.right)
        self.b.wait_recv()
        ref = self.relay(1)
        ref[...] = ref[...] + self.part(self.left, 1)[...]
        self.f = self.go(ref, self.landing(1, 1), self.left)

    def finish(self, half):
        for copy in (self.d, self.e) if half == 0 else (self.c, self.f):
            copy.wait_recv()
        return self.part(self.me, half)[...] + (self.landing(0, half)[...] + self.landing(1, half)[...])


class RingGather:
    def __init__(self, links, me, to, part, group, first, rest):
        self.links, self.me, self.to, self.part = links, me, to, part
        self.group, self.first, self.rest = group, first, rest
        self.right, self.left = lax.rem(me + 1, 4), lax.rem(me + 3, 4)

    def go(self, place, half, device, arrivals):
        ref = self.part(place, half)
        self.links.start(ref, ref, self.to(device), self.group, arrivals)

    def start(self):
        self.go(self.me, 0, self.right, self.first)
        self.go(self.me, 1, self.left, self.first)
        self.go(self.me, 1, self.right, self.rest)
        self.go(self.me, 0, self.left, self.rest)

    def forward(self):
        self.go(self.left, 0, self.right, self.rest)
        self.go(self.right, 1, self.left, self.rest)


def exchange_kernel(
    momentum, gradient, right_in, right_out, ortho_out, scale_out, momentum_out,
    early, early_g, late_c, late_g, late, rearly, rlate, summed, relay_b, landing_b, relay_a, landing_a,
    part_left, core_in, tiles, tiles_in, tile_out, left_tiles, left_t,
    gram_y, gram_all, chol, chol_x, chol_pivots, part_a, relay_ta, landing_ta, all_a,
    part_b, relay_tb, landing_tb, all_b, squares,
    send, recv, load, many,
):
    x, f, y = lax.axis_index("rep"), lax.axis_index("fsdp"), lax.axis_index("tp")
    z, core = f // 2, lax.rem(f, 2)
    q = x * 8 + z

    def at(x=x, z=z, core=core, y=y):
        return {"rep": x, "fsdp": z * 2 + core, "tp": y}

    def middle_out(i):
        return ((i + 1) // 2) * (1 - 2 * lax.rem(i, 2))

    def plane(i):
        there_x = lax.rem(x + 2 + middle_out(lax.rem(i, 4)), 4)
        there_z = lax.rem(z + 4 + middle_out(i // 4), 8)
        return there_x * 8 + there_z, at(x=there_x, z=there_z)

    to_x = lambda p: at(x=p)
    to_y = lambda p: at(y=p)
    partner = at(core=1 - core)
    links = Links(send, recv)

    barrier = pltpu.get_barrier_semaphore()

    def greet(d, carry):
        pl.semaphore_signal(barrier, inc=1, device_id=plane(d)[1], device_id_type=MESH)
        return carry

    for d in (1, 2, 3):
        pl.semaphore_signal(barrier, inc=1, device_id=to_y(lax.rem(y + d, 4)), device_id_type=MESH)
    pl.semaphore_signal(barrier, inc=1, device_id=partner, device_id_type=MESH)
    lax.fori_loop(0, 31, greet, 0)

    order = [lax.rem(x + d, 4) for d in (2, 1, 3, 0)]
    loads = []
    for i, p in enumerate(order):
        cols = pl.ds(pl.multiple_of(EARLY * p, EARLY), EARLY)
        loads.append(
            (
                pltpu.make_async_copy(momentum.at[:, cols], early.at[p], load.at[2 * i]),
                pltpu.make_async_copy(gradient.at[:, cols], early_g.at[p], load.at[2 * i + 1]),
            )
        )
    loads.append(
        (
            pltpu.make_async_copy(momentum.at[:, EARLY_COLS:COLS], late_c, load.at[8]),
            pltpu.make_async_copy(gradient.at[:, EARLY_COLS:COLS], late_g, load.at[9]),
        )
    )
    for pair in loads[:4]:
        for copy in pair:
            copy.start()

    def loaded(i):
        for copy in loads[i]:
            copy.wait()
        early[order[i]] = early[order[i]] + early_g[order[i]]

    my_ranks = pl.ds(pl.multiple_of(64 * y, 64), 64)
    rearly[my_ranks, :] = right_in[:, pl.ds(pl.multiple_of(EARLY * x, EARLY), EARLY)]
    rlate[my_ranks, :] = right_in[:, EARLY_COLS:COLS]
    loaded(0)
    pl.semaphore_wait(barrier, 35)

    def rank_rows(p, h):
        return pl.ds(pl.multiple_of(64 * p + 32 * h, 32), 32)

    def half(h):
        return slice(128 * h, 128 * (h + 1))

    sum_b = RingSum(
        links, x, to_x, lambda p, h: early.at[p, half(h)],
        lambda h: relay_b.at[h], lambda i, h: landing_b.at[i, h], early.at[0:3],
    )
    gathers = []
    for ref in (rlate, rearly):
        sems = (links.group(ref.at[0:192]), links.arrivals(), links.arrivals())
        gathers.append(RingGather(links, y, to_y, lambda p, h, ref=ref: ref.at[rank_rows(p, h)], *sems))
    gather_a, gather_b = gathers
    sum_b.start_far()
    gather_a.start()
    gather_b.start()
    loaded(1)
    loaded(2)
    sum_b.start_near()
    for copy in loads[4]:
        copy.start()
    loaded(3)
    for copy in loads[4]:
        copy.wait()
    late_c[...] = late_c[...] + late_g[...]
    for p in range(4):
        late[p] = late_c[:, LATE * p : LATE * (p + 1)]
    links.wait(gather_a.first, rlate.at[0:64])
    gather_a.forward()
    sum_b.middle()
    links.wait(gather_b.first, rearly.at[0:64])
    gather_b.forward()
    links.wait(gather_a.rest, rlate.at[0:128])
    total = dot3(late_c[...], rlate[...], ((1,), (1,)))
    links.wait(gather_b.rest, rearly.at[0:128])
    for h in range(2):
        summed[half(h), 0:EARLY] = sum_b.finish(h)
    total = total + dot3(summed[:, 0:EARLY], rearly[...], ((1,), (1,)))
    part_left[0] = total[0:128]
    part_left[1] = total[128:256]

    swap = links.start(part_left.at[1 - core], core_in, partner)
    sum_a = RingSum(
        links, x, to_x, lambda p, h: late.at[p, half(h)],
        lambda h: relay_a.at[h], lambda i, h: landing_a.at[i, h], late.at[0:3],
    )
    swap.wait_recv()
    mine = part_left[core] + core_in[...]
    tiles[0:16] = mine[:, 0:128].reshape(16, 8, 128)
    tiles[16:32] = mine[:, 128:256].reshape(16, 8, 128)

    def scatter(d, carry):
        other, device = plane(d)
        pltpu.make_async_remote_copy(
            src_ref=tiles.at[other], dst_ref=tiles_in.at[d], send_sem=many.at[0],
            recv_sem=many.at[1], device_id=device, device_id_type=MESH,
        ).start()
        return carry

    def gather(d, carry):
        pltpu.make_async_remote_copy(
            src_ref=tile_out, dst_ref=left_tiles.at[core, q], send_sem=many.at[2],
            recv_sem=many.at[3], device_id=plane(d)[1], device_id_type=MESH,
        ).start()
        return carry

    def wait_many(i, ref):
        pltpu.make_async_copy(ref, ref, many.at[i]).wait()

    lax.fori_loop(0, 31, scatter, 0)
    sum_a.start_far()
    wait_many(1, tiles_in)
    tile = (tiles[q] + jnp.sum(tiles_in[...], axis=0)) * 0.25
    tile_out[...] = tile
    left_tiles[core, q] = tile
    lax.fori_loop(0, 31, gather, 0)
    sum_a.start_near()
    sum_a.middle()
    wait_many(3, tiles_in)
    swap = links.start(left_tiles.at[core], left_tiles.at[core], partner)
    swap.wait_recv()
    left = jnp.concatenate(
        [
            jnp.concatenate([left_tiles[h, 0:16].reshape(128, 128), left_tiles[h, 16:32].reshape(128, 128)], axis=1)
            for h in range(2)
        ],
        axis=0,
    )
    left_t[...] = left.T

    def ranks(p, h, part=None):
        n = SHARES[h]
        low, count = ((0, n), (0, n // 16 * 8 + 8), (n // 16 * 8 + 8, n - n // 16 * 8 - 8))[0 if part is None else part + 1]
        return pl.ds(pl.multiple_of((0, 4 * SHARES[0])[h] + n * p + low, 8), count)

    class Product:
        def __init__(self, cols, like, part, relay, landing, whole):
            self.cols, self.like, self.part, self.whole = cols, like, part, whole
            first = (0, SHARES[0])

            def rows(h):
                return slice(first[h], first[h] + SHARES[h])

            self.sum = RingSum(
                links, y, to_y, lambda p, h: part.at[ranks(p, h)],
                lambda h: relay.at[rows(h)], lambda i, h: landing.at[i, rows(h)], like.at[0, 0:192],
            )
            self.group_1, self.group_2 = links.group(like.at[0, 0:192]), links.group(like.at[0:3])
            self.from_place = {d: links.arrivals() for d in (1, 2, 3)}
            self.first = {d: links.arrivals() for d in range(4)}
            self.rest = links.arrivals()
            self.rings = {}

        def multiply(self):
            self.part[...] = dot3(left_t[...], summed[:, self.cols])

        def share(self):
            for h in range(2):
                piece = self.whole.at[x, ranks(y, h)]
                piece[...] = self.sum.finish(h)
                for d in (1, 3, 2):
                    there = to_y(lax.rem(y + d, 4)) if h == 0 else to_x(lax.rem(x + d, 4))
                    links.start(piece, piece, there, self.group_1, self.from_place[4 - d])
            self.pass_on(0)

        def pass_on(self, d):
            whole = self.whole
            from_y, from_x = lax.rem(y + d, 4), lax.rem(x + d, 4)
            sems = (self.group_2, self.first[d], self.rest)
            self.rings[d] = (
                RingGather(links, x, to_x, lambda p, i: whole.at[p, ranks(from_y, 0, i)], *sems),
                RingGather(links, y, to_y, lambda p, i: whole.at[from_x, ranks(p, 1, i)], *sems),
            )
            for ring in self.rings[d]:
                ring.start()

        def arrived(self, *places):
            for d in places:
                links.wait(self.from_place[d], self.like.at[0, 0:64])
                self.pass_on(d)

        def forward(self, *places):
            for d in places:
                links.wait(self.first[d], self.like.at[0, 0:64])
                for ring in self.rings[d]:
                    ring.forward()

        def finish(self):
            links.wait(self.rest, self.like.at[0:2])

    a = Product(slice(0, EARLY), early, part_a, relay_ta, landing_ta, all_a)
    b = Product(slice(EARLY, CHUNK), late, part_b, relay_tb, landing_tb, all_b)
    a.multiply()
    a.sum.start()
    slab = left_t[pl.ds(pl.multiple_of((core * 4 + x) * 32, 32), 32), :]
    gram_y[y] = dot(slab, left, precision=HIGHEST)
    grams = [links.start(gram_y.at[y], gram_y.at[y], to_y(lax.rem(y + d, 4))) for d in (2, 1, 3)]
    for h in range(2):
        summed[half(h), EARLY:CHUNK] = sum_a.finish(h)
    b.multiply()
    b.sum.start()
    a.sum.middle()
    for copy in grams:
        copy.wait_recv()
    gram_all[core, x] = (gram_y[0] + gram_y[1]) + (gram_y[2] + gram_y[3])
    grams = [links.start(gram_all.at[core, x], gram_all.at[core, x], to_x(lax.rem(x + d, 4))) for d in (2, 1, 3)]
    b.sum.middle()
    a.share()
    for copy in grams:
        copy.wait_recv()
    swap = links.start(gram_all.at[core], gram_all.at[core], partner)
    b.share()
    swap.wait_recv()
    for c in range(2):
        for p in range(4):
            chol[128 * c + 32 * p : 128 * c + 32 * p + 32, :] = gram_all[c, p]
    pieces = cholesky_pieces(chol, chol_x, chol_pivots)
    once = jnp.minimum(x + 1, 1)

    def work(n):
        now = [pieces.pop(0) for _ in range(n)]

        def step(i, carry):
            for piece in now:
                piece()
            return carry

        lax.fori_loop(0, once, step, 0)

    work(3)
    a.arrived(1, 3)
    work(3)
    b.arrived(1, 3)
    a.forward(0)
    a.arrived(2)
    work(3)
    b.arrived(2)
    b.forward(0)
    work(5)
    a.forward(1, 3)
    b.forward(1, 3)
    work(6)
    a.forward(2)
    b.forward(2)
    work(len(pieces))
    inverse = chol[...]
    ortho = dot(left, inverse, ((1,), (1,)), HIGHEST)
    ortho_out[...] = ortho

    ih, il = split(inverse * 0.25)
    sums = jnp.zeros((ROWS, 1), F32)
    for product, first, width in ((a, 0, EARLY), (b, EARLY_COLS, LATE)):
        product.finish()
        for p in range(4):
            th, tl = split(product.whole[p])
            right = dot(ih, th) + (dot(ih, tl) + dot(il, th))
            right_out[:, first + width * p : first + width * (p + 1)] = right
            sums = sums + jnp.sum(right * right, axis=1, keepdims=True)
    squares[f] = jnp.broadcast_to(sums, (ROWS, 128)).T[0:1]

    def share(i, carry):
        there = at(z=lax.rem(z + 4 + middle_out(i // 2), 8), core=lax.rem(core + 1 + i, 2))
        pltpu.make_async_remote_copy(
            src_ref=squares.at[f], dst_ref=squares.at[f], send_sem=many.at[4],
            recv_sem=many.at[5], device_id=there, device_id_type=MESH,
        ).start()
        return carry

    lax.fori_loop(0, 15, share, 0)
    basis = ortho.astype(BF16)
    rate = 1.0 - momentum_decay
    for p in range(4):
        cols = slice(EARLY * p, EARLY * (p + 1))
        momentum_out[:, cols] = early[p] - rate * dot(basis, right_out[:, cols].astype(BF16))
    cols = slice(EARLY_COLS, COLS)
    momentum_out[:, cols] = late_c[...] - rate * dot(basis, right_out[:, cols].astype(BF16))
    wait_many(5, squares.at[0:15])
    total = jnp.sum(squares[...], axis=0)
    scale_out[...] = jnp.broadcast_to(lax.rsqrt(total / TOTAL_COLS + norm_eps), (8, ROWS))
    wait_many(0, tiles_in)
    wait_many(2, tiles_in)
    wait_many(4, squares.at[0:15])
    links.drain()
    assert links.sends <= SENDS and links.recvs <= ARRIVALS


def exchange(momentum, gradient, right_t):
    vmem = lambda *shape: pltpu.VMEM(shape, F32)
    return pl.pallas_call(
        exchange_kernel,
        out_shape=(
            jax.ShapeDtypeStruct((ROWS, COLS), F32),
            jax.ShapeDtypeStruct((ROWS, ROWS), F32),
            jax.ShapeDtypeStruct((8, ROWS), F32),
            jax.ShapeDtypeStruct((ROWS, COLS), F32),
        ),
        in_specs=[pl.BlockSpec(memory_space=pltpu.HBM)] * 2 + [pl.BlockSpec(memory_space=pltpu.VMEM)],
        out_specs=(pl.BlockSpec(memory_space=pltpu.VMEM),) * 4,
        scratch_shapes=[
            vmem(4, ROWS, EARLY),
            vmem(4, ROWS, EARLY),
            vmem(ROWS, LATE_COLS),
            vmem(ROWS, LATE_COLS),
            vmem(4, ROWS, LATE),
            vmem(ROWS, EARLY),
            vmem(ROWS, LATE_COLS),
            vmem(ROWS, CHUNK),
            vmem(2, 128, EARLY),
            vmem(2, 2, 128, EARLY),
            vmem(2, 128, LATE),
            vmem(2, 2, 128, LATE),
            vmem(2, 128, ROWS),
            vmem(128, ROWS),
            vmem(32, 8, 128),
            vmem(31, 8, 128),
            vmem(8, 128),
            vmem(2, 32, 8, 128),
            vmem(ROWS, ROWS),
            vmem(4, 32, ROWS),
            vmem(2, 4, 32, ROWS),
            vmem(ROWS, ROWS),
            vmem(NB, 128),
            vmem(NB, 128),
            vmem(ROWS, EARLY),
            vmem(64, EARLY),
            vmem(2, 64, EARLY),
            vmem(4, ROWS, EARLY),
            vmem(ROWS, LATE),
            vmem(64, LATE),
            vmem(2, 64, LATE),
            vmem(4, ROWS, LATE),
            vmem(16, 1, ROWS),
            pltpu.SemaphoreType.DMA((SENDS,)),
            pltpu.SemaphoreType.DMA((ARRIVALS,)),
            pltpu.SemaphoreType.DMA((10,)),
            pltpu.SemaphoreType.DMA((6,)),
        ],
        compiler_params=pltpu.CompilerParams(
            collective_id=0, has_side_effects=True, vmem_limit_bytes=45 * 1024 * 1024
        ),
        cost_estimate=pl.CostEstimate(flops=4 * 2 * ROWS * ROWS * COLS, bytes_accessed=11_000_000, transcendentals=0),
        name="exchange",
    )(momentum, gradient, right_t)


def update_kernel(
    ortho, scale, right, weights, momentum, new_weights, new_momentum, new_right, staged_w, column_ref, staged_r, sems
):
    copies = [pltpu.make_async_copy(momentum, new_momentum, sems.at[0])]
    copies[0].start()
    own = pl.ds(pl.multiple_of(lax.axis_index("tp") * 64, 64), 64)
    sh, sl = split(ortho[...] * scale[0:1, :])
    column_ref[...] = jnp.broadcast_to(scale[0:1, :], (128, ROWS)).T
    column = column_ref[own, :]
    for i, (low, high) in enumerate(zip(EDGES[:-1], EDGES[1:])):
        cols = slice(low, high)
        rh, rl = split(right[:, cols])
        normal = dot(sh, rh) + (dot(sh, rl) + dot(sl, rh))
        staged_w[:, cols] = weights[:, cols] - learning_rate * normal
        staged_r[:, cols] = jnp.concatenate([column] * ((high - low) // 128), axis=1) * right[own, cols]
        copies.append(pltpu.make_async_copy(staged_w.at[:, cols], new_weights.at[:, cols], sems.at[2 * i + 1]))
        copies[-1].start()
        copies.append(
            pltpu.make_async_copy(staged_r.at[:, cols], new_right.at[:, cols], sems.at[2 * i + 2])
        )
        copies[-1].start()
    for copy in copies:
        copy.wait()


EDGES = (0, 1280, 2304, 3072, 3328)


def update(ortho, scale, right, weights, momentum):
    return pl.pallas_call(
        update_kernel,
        out_shape=(
            jax.ShapeDtypeStruct((ROWS, COLS), F32),
            jax.ShapeDtypeStruct((ROWS, COLS), F32),
            jax.ShapeDtypeStruct((64, COLS), F32),
        ),
        in_specs=[pl.BlockSpec(memory_space=pltpu.VMEM)] * 5,
        out_specs=(pl.BlockSpec(memory_space=pltpu.HBM),) * 3,
        scratch_shapes=[
            pltpu.VMEM((ROWS, COLS), F32),
            pltpu.VMEM((ROWS, 128), F32),
            pltpu.VMEM((64, COLS), F32),
            pltpu.SemaphoreType.DMA((2 * len(EDGES) - 1,)),
        ],
        compiler_params=pltpu.CompilerParams(vmem_limit_bytes=40 * 1024 * 1024),
        name="update",
    )(ortho, scale, right, weights, momentum)


def local(weights, momentum, gradient, right_factor):
    right, ortho, scale, moved = exchange(momentum, gradient, right_factor.T)
    new_weights, new_momentum, new_right_t = update(ortho, scale, right, weights, moved)
    return (new_weights, new_momentum, new_right_t.T)


def solution(mesh):
    return jax.shard_map(
        local,
        mesh=mesh,
        in_specs=(
            P("tp", "fsdp"),
            P(("rep", "tp"), "fsdp"),
            P(("rep", "tp"), "fsdp"),
            P("fsdp", "tp"),
        ),
        out_specs=(P("tp", "fsdp"), P(("rep", "tp"), "fsdp"), P("fsdp", "tp")),
        check_vma=False,
    )
```
